128 devices in a mesh: row: 8 (over y_hi, x), col: 16 (over y_lo, z, core).
Axes of the slice: x: 4, y: 4 (y_hi: 2, y_lo: 2; y = y_hi * 2 + y_lo), z: 4, core: 2. Of those that a mesh axis runs over, the one named last changes fastest.
Arguments:
- top_coeffs: float32 [8, 131072], P(None, ('row', 'col')), may hold values from -6 to 6
- fresh_one: bfloat16 [56, 131072], P(None, ('row', 'col')), may hold values from -6 to 6
- fresh_two: bfloat16 [56, 8, 131072], P(None, None, ('row', 'col')), may hold values from -6 to 6
- fresh_three: bfloat16 [56, 64, 131072], P(None, None, ('row', 'col')), may hold values from -6 to 6
- mixing: bfloat16 [64, 64], replicated, may hold values from -0.75 to 0.75
- transfer: float32 [2048, 2048], P(None, 'col'), may hold values from 0.1 to 1, as said below
Outputs:
- density: float32 [16, 2048, 2048], P('row', 'col')
The draws below stay inside these ranges and needn't reach their ends.
Inputs may be any that keep to these rules, and one draw needn't show every extreme that they name: transfer is even: its value at the positions of modes (ky, kz) equals its value at the positions of modes (-ky mod 2048, -kz mod 2048).
All inputs are finite; a program needn't handle non-finite values.
Results may differ from the reference program's by a relative error of at most 0.0003.
Values sent between devices are 32-bit elements; how exact they have to be, the bound alone decides.
A program may use at most 192 MiB of HBM per device.

```python
import math
import jax
import jax.numpy as jnp
import numpy as np
from jax import lax

NG = 2048
PLANES = 16
BLOCKS = 256
NBLK = 131072
SLOTS = 1024
N_ROW = 8
N_COL = 16


def draw_transfer(key, part):
    base = jnp.exp(jax.random.uniform(key, (NG, NG), jnp.float32, math.log(0.1), 0.0))
    mirrored = jnp.roll(base[::-1, ::-1], (1, 1), axis=(0, 1))
    natural = 0.5 * (base + mirrored)
    major = NG // 128
    return natural.reshape(128, major, 128, major).transpose(1, 0, 3, 2).reshape(NG, NG).astype(jnp.float32)


def level_of(own_key, shape, pieces, smallest, high):
    def one(position, blocks):
        draws = jax.random.uniform(jax.random.fold_in(jax.random.fold_in(own_key, 6), position), (blocks,), jnp.float32, smallest / len(pieces), high / len(pieces))
        return jnp.repeat(jnp.exp(draws), shape[position] // blocks).reshape((-1,) + (1,) * (len(shape) - position - 1))

    level = one(*pieces[0])
    for cut in pieces[1:]:
        level = level * one(*cut)
    return level


def bell_draw(own_key, shape, scale, limit, split=(), held_as=jnp.bfloat16):
    values = scale * jax.random.normal(own_key, shape, jnp.float32)
    if split:
        values = values * level_of(own_key, shape, split, -0.22, 0.18)
    return jnp.clip(values, -limit, limit).astype(held_as)


def setup_inputs(seed: int = 0) -> dict:
    keys = jax.random.split(jax.random.key(seed), 7)
    return {
        "top_coeffs": bell_draw(keys[0], (8, NBLK), 1.0, 6.0, ((1, 128),), jnp.float32),
        "fresh_one": bell_draw(keys[1], (56, NBLK), 1.0, 6.0, ((1, 128),)),
        "fresh_two": bell_draw(keys[2], (56, 8, NBLK), 1.0, 6.0, ((2, 128),)),
        "fresh_three": bell_draw(keys[3], (56, 64, NBLK), 1.0, 6.0, ((2, 128),)),
        "mixing": bell_draw(keys[4], (64, 64), 64 ** -0.5, 0.75),
        "transfer": draw_transfer(jax.random.fold_in(keys[6], 71), 0),
    }


def expand_level(parents, fresh, mixing, full):
    rows = mixing if full else mixing[0::8]
    count = rows.shape[0]
    cells = parents.shape[1]
    blocks = parents.shape[2]
    carried = jnp.einsum("ij,jcb->icb", rows[:, :8].astype(jnp.float32), parents, precision=lax.Precision.HIGHEST)
    drawn = jnp.einsum("ij,jcb->icb", rows[:, 8:].astype(jnp.float32), fresh.astype(jnp.float32), precision=lax.Precision.HIGHEST)
    total = carried + drawn
    if full:
        return total.reshape(8, 8, cells, blocks).transpose(1, 2, 0, 3).reshape(8, cells * 8, blocks)
    return total.transpose(1, 0, 2).reshape(cells * 8, blocks)


def record_table(block_count, n_row, n_col):
    owners = n_row * n_col
    per_strip = block_count // n_col
    y_bits = per_strip.bit_length() - 1
    class_slots = per_strip * block_count // owners
    slot_count = 2 * n_col * class_slots
    x_half, y_block, z_block = np.meshgrid(np.arange(2), np.arange(block_count), np.arange(block_count), indexing="ij")
    strip = y_block // per_strip
    y_local = y_block % per_strip
    code = z_block * 0
    for bit_index in range(y_bits):
        code = code + (((z_block >> bit_index) & 1) << (2 * bit_index))
        code = code + (((y_local >> bit_index) & 1) << (2 * bit_index + 1))
    code = code + ((z_block >> y_bits) << (2 * y_bits))
    owner = code % owners
    inner = code // owners
    record = owner * slot_count + (x_half * n_col + strip) * class_slots + inner
    return record.astype(np.int32)


def reference(top_coeffs, fresh_one, fresh_two, fresh_three, mixing, transfer):
    owners = N_ROW * N_COL

    def leaves_of(index):
        start = index * SLOTS
        top = lax.dynamic_slice_in_dim(top_coeffs, start, SLOTS, 1)
        first = lax.dynamic_slice_in_dim(fresh_one, start, SLOTS, 1)
        second = lax.dynamic_slice_in_dim(fresh_two, start, SLOTS, 2)
        third = lax.dynamic_slice_in_dim(fresh_three, start, SLOTS, 2)
        level = expand_level(top[:, None, :], first[:, None, :], mixing, True)
        level = expand_level(level, second, mixing, True)
        return expand_level(level, third, mixing, False)

    leaves = lax.map(leaves_of, jnp.arange(owners, dtype=jnp.int32))
    records = leaves.transpose(0, 2, 1).reshape(NBLK, 512)
    table = jnp.asarray(record_table(BLOCKS, N_ROW, N_COL)).astype(jnp.int32)
    grid = jnp.take(records, table, axis=0)
    grid = grid.reshape((2, BLOCKS, BLOCKS) + (2,) * 9)
    field = grid.transpose(0, 3, 6, 9, 1, 4, 7, 10, 2, 5, 8, 11).reshape(PLANES, NG, NG)
    spectrum = jnp.fft.fft2(field, axes=(1, 2))
    major = NG // 128
    natural = transfer.reshape(major, 128, major, 128).transpose(1, 0, 3, 2).reshape(NG, NG)
    result = jnp.fft.ifft2(spectrum * natural, axes=(1, 2))
    return jnp.real(result).astype(jnp.float32)
```

```python
import functools
import math

import jax
import jax.numpy as jnp
import numpy as np
from jax import lax
from jax.experimental import pallas as pl
from jax.experimental.pallas import tpu as pltpu
from jax.sharding import PartitionSpec as P

F32 = jnp.float32
BF16 = jnp.bfloat16
VMEM = pltpu.VMEM


def two_terms(values):
    values = np.asarray(values, np.float32)
    high = values.astype(jnp.bfloat16)
    low = (values - high.astype(np.float32)).astype(jnp.bfloat16)
    return high, low


def bit(value, index):
    return (value >> index) & 1


def owner_tables():
    row = np.arange(64)
    pick_one = np.zeros((64, 64), np.float32)
    pick_one[row, 8 * (row % 8) + row // 8] = 1
    row = np.arange(512)
    cell, coef, parent = row % 8, (row >> 4) & 7, 2 * (row >> 7) + bit(row, 3)
    pick_two = np.zeros((512, 64), np.float32)
    pick_two[row, 8 * cell + coef] = 1
    column = np.arange(512)
    source = np.where(column < 448, 8 + column // 8, (column - 448) // 8)
    spread_two = np.zeros((64, 512), np.float32)
    spread_two[source, column] = 1
    mask_two = (column[None, :] % 8 == parent[:, None]).astype(np.float32)
    row = np.arange(128)
    c2x, c3x, c2y, c3y, c1z, c2z, c3z = [bit(row, 6 - i) for i in range(7)]
    pick_three = np.zeros((128, 64), np.float32)
    pick_three[row, 8 * (4 * c3x + 2 * c3y + c3z)] = 1
    column = np.arange(1024)
    source = np.where(column < 896, 8 + column // 16, (column - 896) // 16)
    spread_three = np.zeros((64, 1024), np.float32)
    spread_three[source, column] = 1
    own = 8 * c1z + 4 * c2x + 2 * c2y + c2z
    mask_three = (column[None, :] % 16 == own[:, None]).astype(np.float32)
    picks = [pick_one, pick_two, spread_two, mask_two, pick_three, spread_three, mask_three]
    return [np.asarray(each, jnp.bfloat16) for each in picks]


def slot_tables():
    slot = np.arange(128)
    y_part = 2 * (slot // 32) + slot % 2
    z_part = (slot // 2) % 16
    mode = np.arange(128)
    kz, ky = mode // 8, mode % 8
    angle = 2 * np.pi * (np.outer(kz, z_part) / 16 + np.outer(ky, y_part) / 8)
    high, low = two_terms(np.concatenate([np.cos(angle), np.sin(angle)], axis=1))
    both = np.concatenate([high, low], axis=0)
    turn = 2 * np.pi * np.outer(np.arange(4), y_part) / 32
    turns = np.stack([np.cos(turn), np.sin(turn)]).astype(np.float32)
    return both, turns


def line_tables():
    z_low = np.arange(128)
    out = []
    for kz_low in range(16):
        angle = 2 * np.pi * np.outer(z_low, kz_low + 16 * np.arange(128)) / 2048
        cos, sin = np.cos(angle), np.sin(angle)
        out.append(np.block([[cos, -sin], [sin, cos]]))
    return np.stack(two_terms(np.stack(out)), axis=1)


def turn_tables():
    kt = np.arange(4)[:, None]
    s = np.arange(8)[None, :]
    ky_low = kt + 4 * s
    one = 2 * np.pi * ky_low[:, None, :] * np.arange(8)[None, :, None] / 256
    mode = ky_low[:, None, None, :] + 32 * np.arange(8)[None, None, :, None]
    two = 2 * np.pi * mode * np.arange(8)[None, :, None, None] / 2048
    wide = lambda a: np.ascontiguousarray(
        np.broadcast_to(np.stack([np.cos(a), np.sin(a)])[..., None], (2,) + a.shape + (128,))
    ).astype(np.float32)
    return wide(one), wide(two)


def digit_tables():
    out = []
    for pair in range(2):
        full = np.zeros((2, 2, 8, 8, 2, 2, 8, 8))
        for k in range(2):
            y2a = np.arange(8)[:, None]
            s = np.arange(8)[None, :]
            angle = 2 * np.pi * (s * y2a / 8 + (2 * pair + k) * y2a / 32)
            cos, sin = np.cos(angle), np.sin(angle)
            for y0 in range(8):
                full[0, k, :, y0, 0, k, y0, :] = cos
                full[0, k, :, y0, 1, k, y0, :] = -sin
                full[1, k, :, y0, 0, k, y0, :] = sin
                full[1, k, :, y0, 1, k, y0, :] = cos
        high, low = two_terms(full.reshape(256, 256))
        out.append(np.concatenate([high, low], axis=0))
    return np.stack(out)


def split(x):
    high = x.astype(BF16)
    return high, (x - high.astype(F32)).astype(BF16)


def dot(a, b):
    return jnp.dot(a, b, preferred_element_type=F32)


def dot_nt(a, b):
    return lax.dot_general(a, b, (((1,), (1,)), ((), ())), preferred_element_type=F32)


def add(a, b):
    return (a[0] + b[0], a[1] + b[1])


def sub(a, b):
    return (a[0] - b[0], a[1] - b[1])


def times(a, cos, sin, sign):
    if sign > 0:
        return (a[0] * cos - a[1] * sin, a[1] * cos + a[0] * sin)
    return (a[0] * cos + a[1] * sin, a[1] * cos - a[0] * sin)


def quarter(a, sign):
    return (-a[1], a[0]) if sign > 0 else (a[1], -a[0])


def add_quarter(a, b, sign):
    return (a[0] - b[1], a[1] + b[0]) if sign > 0 else (a[0] + b[1], a[1] - b[0])


def four(x, sign):
    even, odd = add(x[0], x[2]), add(x[1], x[3])
    left, right = sub(x[0], x[2]), sub(x[1], x[3])
    return [add(even, odd), add_quarter(left, right, sign), sub(even, odd),
            add_quarter(left, right, -sign)]


def eight(x, sign):
    even = four([x[0], x[2], x[4], x[6]], sign)
    odd = four([x[1], x[3], x[5], x[7]], sign)
    half = math.sqrt(0.5)
    a = odd[1]
    if sign > 0:
        odd1 = ((a[0] - a[1]) * half, (a[1] + a[0]) * half)
    else:
        odd1 = ((a[0] + a[1]) * half, (a[1] - a[0]) * half)
    a = odd[3]
    if sign > 0:
        odd3 = ((-a[0] - a[1]) * half, (a[0] - a[1]) * half)
    else:
        odd3 = ((a[1] - a[0]) * half, (-a[0] - a[1]) * half)
    return [
        add(even[0], odd[0]),
        add(even[1], odd1),
        add_quarter(even[2], odd[2], sign),
        add(even[3], odd3),
        sub(even[0], odd[0]),
        sub(even[1], odd1),
        add_quarter(even[2], odd[2], -sign),
        sub(even[3], odd3),
    ]


def sixteen(x, sign):
    out = [None] * 16
    mid = [four([x[a], x[a + 4], x[a + 8], x[a + 12]], sign) for a in range(4)]
    for c in range(4):
        terms = []
        for a in range(4):
            angle = 2 * math.pi * a * c / 16
            if a * c == 0:
                terms.append(mid[a][c])
            elif a * c == 4:
                terms.append(quarter(mid[a][c], sign))
            else:
                terms.append(times(mid[a][c], math.cos(angle), math.sin(angle), sign))
        done = four(terms, sign)
        for d in range(4):
            out[c + 4 * d] = done[d]
    return out


def owner_kernel(top, one, two, three, mixing, pick_one, pick_two, spread_two, mask_two,
                 pick_three, spread_three, mask_three, slots, turns, out,
                 parents, leaf_map, leaves, high_rows, low_rows):
    step = pl.program_id(0)

    @pl.when(step == 0)
    def _():
        mix = mixing[...]
        first = dot(pick_one[...], mix).astype(BF16)
        high, low = split(jnp.concatenate([top[...], one[...].astype(F32)], axis=0))
        level_one = dot(first, high) + dot(first, low)
        rows = dot(pick_two[...], mix).astype(BF16)
        second = (dot(rows, spread_two[...]) * mask_two[...].astype(F32)).astype(BF16)
        high, low = split(level_one)
        level_two = dot(second, jnp.concatenate([two[...], high], axis=0))
        level_two = level_two + dot(second[:, 384:], jnp.concatenate([jnp.zeros_like(low), low], axis=0))
        for tile in range(4):
            high, low = split(level_two[tile * 128:(tile + 1) * 128])
            parents[tile, 0:128] = high
            parents[tile, 128:256] = low
        rows = dot(pick_three[...], mix).astype(BF16)
        leaf_map[...] = (dot(rows, spread_three[...]) * mask_three[...].astype(F32)).astype(BF16)

    draws = three[...].reshape(896, 1024)
    got = dot(leaf_map[:, :896], draws)
    near = parents[step]
    got = got + dot(leaf_map[:, 896:], near[:128]) + dot(leaf_map[:, 896:], near[128:])
    half = lax.rem(step, 2)
    for group in range(4):
        leaves[group, half] = got[group * 32:(group + 1) * 32]

    @pl.when(half == 1)
    def _():
        for e in range(2):
            for pair in range(2):
                quarters = []
                for t in range(4):
                    lane = (4 * e + t) * 128
                    re = leaves[2 * pair, :, :, lane:lane + 128].reshape(64, 128)
                    im = leaves[2 * pair + 1, :, :, lane:lane + 128].reshape(64, 128)
                    quarters.append((re, im))
                for k, value in enumerate(four(quarters, -1)):
                    if k:
                        value = times(value, turns[0, k:k + 1], turns[1, k:k + 1], -1)
                    re_high, re_low = split(value[0])
                    im_high, im_low = split(value[1])
                    base = pair * 128
                    high_rows[k, base:base + 64, 0:128] = re_high
                    high_rows[k, base:base + 64, 128:256] = im_high
                    high_rows[k, base + 64:base + 128, 0:128] = im_high
                    high_rows[k, base + 64:base + 128, 128:256] = -re_high
                    low_rows[k, base:base + 64, 0:128] = re_low
                    low_rows[k, base:base + 64, 128:256] = im_low
                    low_rows[k, base + 64:base + 128, 0:128] = im_low
                    low_rows[k, base + 64:base + 128, 128:256] = -re_low
            for k in range(4):
                both = dot_nt(slots[...], high_rows[k])
                done = both[:128] + both[128:] + dot_nt(slots[0:128], low_rows[k])
                for pair in range(2):
                    place = 4 * e + 2 * (step // 2) + pair
                    piece = done[:, pair * 128:(pair + 1) * 128].reshape(16, 8, 128)
                    out[place, :, k] = piece


def owners(top, one, two, three, mixing):
    tables = owner_tables()
    slots, turns = slot_tables()
    whole = lambda a: pl.BlockSpec(a.shape, lambda i: (0,) * a.ndim)
    two = two.reshape(448, 1024)
    operands = [top, one, two, three, mixing] + [jnp.asarray(t) for t in tables]
    operands += [jnp.asarray(slots), jnp.asarray(turns)]
    specs = [whole(a) for a in operands]
    specs[3] = pl.BlockSpec((56, 16, 1024), lambda i: (0, i, 0))
    return pl.pallas_call(
        owner_kernel,
        grid=(4,),
        in_specs=specs,
        out_specs=pl.BlockSpec((8, 16, 4, 8, 128), lambda i: (0, 0, 0, 0, 0)),
        out_shape=jax.ShapeDtypeStruct((8, 16, 4, 8, 128), F32),
        scratch_shapes=[
            VMEM((4, 256, 1024), BF16),
            VMEM((128, 1024), BF16),
            VMEM((4, 2, 32, 1024), F32),
            VMEM((4, 256, 256), BF16),
            VMEM((4, 256, 256), BF16),
        ],
        compiler_params=pltpu.CompilerParams(vmem_limit_bytes=56 * 2**20),
    )(*operands)


def owner_index(q, w):
    index = 0
    for b in range(4):
        index += bit(w, b) << (2 * b)
    for b in range(3):
        index += bit(q, b) << (2 * b + 1)
    return index


def swap_lanes(x, lane):
    for b in range(4):
        width = 8 << b
        keep = (lane & width) == 0
        y = list(x)
        for i in range(16):
            if not bit(i, b):
                j = i | (1 << b)
                y[i] = jnp.where(keep, x[i], pltpu.roll(x[j], width, 1))
                y[j] = jnp.where(keep, pltpu.roll(x[i], 128 - width, 1), x[j])
        x = y
    return x


def line_kernel(arrived, transfer, lines, turn_one, turn_two, digits, out,
                factor, table, sem, flat, mid, work, spread, lined):
    col = lax.axis_index("col")
    fetch = pltpu.make_async_copy(lines.at[col], table, sem)
    fetch.start()

    @pl.loop(0, 128)
    def _(i):
        low, kt, high = i // 32, (i // 8) % 4, i % 8
        rows = transfer[pl.ds(pl.multiple_of((low * 4 + kt) * 128 + high * 16, 16), 16), :]
        factor[pl.ds((kt * 8 + high) * 64 + low, 16, stride=4), :] = rows * (1.0 / (2048 * 2048))

    fetch.wait()
    lane = lax.broadcasted_iota(jnp.int32, (8, 128), 1)

    @pl.loop(0, 4)
    def _(kt):
        for q in range(8):
            got = swap_lanes([arrived[owner_index(q, w), kt] for w in range(16)], lane)
            for oy in range(8):
                flat[pl.ds((q * 8 + oy) * 8, 8), 0:128] = got[oy]
                flat[pl.ds((q * 8 + oy) * 8, 8), 128:256] = got[8 + oy]
        for part in range(2):
            rows = pl.ds(part * 256, 256)
            high, low = split(flat[rows, :])
            mid[rows, :] = dot(high, table[0]) + dot(low, table[0]) + dot(high, table[1])

        @pl.loop(0, 8)
        def _(oy):
            x = []
            for q in range(8):
                rows = pl.ds(pl.multiple_of(q * 64 + oy * 8, 8), 8)
                value = (mid[rows, 0:128], mid[rows, 128:256])
                if q:
                    value = times(value, turn_one[0, kt, q], turn_one[1, kt, q], -1)
                x.append(value)
            for k, value in enumerate(eight(x, -1)):
                value = times(value, turn_two[0, kt, oy, k], turn_two[1, kt, oy, k], -1)
                work[0, k, oy] = value[0]
                work[1, k, oy] = value[1]

        @pl.loop(0, 8)
        def _(kq):
            x = eight([(work[0, kq, oy], work[1, kq, oy]) for oy in range(8)], -1)
            y = []
            for k in range(8):
                rows = pl.ds(pl.multiple_of((kt * 8 + k) * 64 + kq * 8, 8), 8)
                scale = factor[rows, :]
                y.append((x[k][0] * scale, x[k][1] * scale))
            for y0, value in enumerate(eight(y, 1)):
                value = times(value, turn_two[0, kt, y0, kq], turn_two[1, kt, y0, kq], 1)
                work[0, kq, y0] = value[0]
                work[1, kq, y0] = value[1]

        @pl.loop(0, 8)
        def _(y0):
            x = [(work[0, kq, y0], work[1, kq, y0]) for kq in range(8)]
            for y1, value in enumerate(eight(x, 1)):
                if y1:
                    value = times(value, turn_one[0, kt, y1], turn_one[1, kt, y1], 1)
                spread[0, kt, y1, y0] = value[0]
                spread[1, kt, y1, y0] = value[1]

    @pl.loop(0, 4)
    def _(pair):
        got = []
        for ktp in range(2):
            columns = []
            for one in range(2):
                pieces = [
                    spread[part, 2 * ktp + k, 2 * pair + one].reshape(64, 128)
                    for part in range(2)
                    for k in range(2)
                ]
                columns.append(jnp.concatenate(pieces, axis=0))
            high, low = split(jnp.concatenate(columns, axis=1))
            both = dot(digits[ktp], high)
            got.append(both[:256] + both[256:] + dot(digits[ktp, 0:256], low))
        for y2a in range(8):
            for one in range(2):
                x = []
                for kt in range(4):
                    base = (kt % 2) * 64 + y2a * 8
                    tile = got[kt // 2]
                    lanes = slice(one * 128, one * 128 + 128)
                    x.append((tile[base:base + 8, lanes], tile[128 + base:128 + base + 8, lanes]))
                for y2b, value in enumerate(four(x, 1)):
                    rows = pl.ds(pl.multiple_of((y2b * 8 + y2a) * 64 + (2 * pair + one) * 8, 8), 8)
                    lined[rows, 0:128] = value[0]
                    lined[rows, 128:256] = value[1]

    @pl.loop(0, 8)
    def _(chunk):
        high, low = split(lined[pl.ds(pl.multiple_of(chunk * 256, 256), 256), :])
        done = dot_nt(high, table[0]) + dot_nt(low, table[0]) + dot_nt(high, table[1])
        for half in range(2):
            for part in range(2):
                out[2 * chunk + half, part] = done[half * 128:half * 128 + 128,
                                                   part * 128:part * 128 + 128]


def along_lines(arrived, transfer):
    lines = jnp.asarray(line_tables())
    turn_one, turn_two = (jnp.asarray(t) for t in turn_tables())
    digits = jnp.asarray(digit_tables())
    inside = pl.BlockSpec(memory_space=VMEM)
    return pl.pallas_call(
        line_kernel,
        in_specs=[inside, inside, pl.BlockSpec(memory_space=pl.ANY), inside, inside, inside],
        out_specs=inside,
        out_shape=jax.ShapeDtypeStruct((16, 2, 128, 128), F32),
        scratch_shapes=[
            VMEM((2048, 128), F32),
            VMEM((2, 256, 256), BF16),
            pltpu.SemaphoreType.DMA,
            VMEM((512, 256), F32),
            VMEM((512, 256), F32),
            VMEM((2, 8, 8, 8, 128), F32),
            VMEM((2, 4, 8, 8, 8, 128), F32),
            VMEM((2048, 256), F32),
        ],
        compiler_params=pltpu.CompilerParams(vmem_limit_bytes=56 * 2**20),
    )(arrived, transfer, lines, turn_one, turn_two, digits)


def strip_kernel(arrived, out):
    @pl.loop(0, 16)
    def _(tile):
        rows = pl.ds(pl.multiple_of(tile * 8, 8), 8)
        x = [(arrived[k, 0, rows, :], arrived[k, 1, rows, :]) for k in range(16)]
        for z, value in enumerate(sixteen(x, 1)):
            out[0, rows, z * 128:(z + 1) * 128] = value[0]
            out[1, rows, z * 128:(z + 1) * 128] = value[1]


def strips(arrived):
    inside = pl.BlockSpec(memory_space=VMEM)
    return pl.pallas_call(
        strip_kernel,
        in_specs=[inside],
        out_specs=inside,
        out_shape=jax.ShapeDtypeStruct((2, 128, 2048), F32),
        compiler_params=pltpu.CompilerParams(vmem_limit_bytes=32 * 2**20),
    )(arrived)


def body(top, one, two, three, mixing, transfer):
    sent = owners(top, one, two, three, mixing).reshape(128, 32, 128)
    arrived = lax.all_to_all(sent, ("row", "col"), split_axis=0, concat_axis=0, tiled=True)
    lines = along_lines(arrived.reshape(128, 4, 8, 128), transfer)
    back = lax.all_to_all(lines, "col", split_axis=0, concat_axis=0, tiled=True)
    return strips(back)


def solution(mesh):
    return jax.shard_map(
        body,
        mesh=mesh,
        in_specs=(
            P(None, ("row", "col")),
            P(None, ("row", "col")),
            P(None, None, ("row", "col")),
            P(None, None, ("row", "col")),
            P(),
            P(None, "col"),
        ),
        out_specs=P("row", "col", None),
        check_vma=False,
    )
```

```python
import math

import jax
import jax.numpy as jnp
import numpy as np
from jax import lax
from jax.experimental import pallas as pl
from jax.experimental.pallas import tpu as pltpu
from jax.sharding import PartitionSpec as P

F32 = jnp.float32
BF16 = jnp.bfloat16
VMEM = pltpu.VMEM
MESH = pl.DeviceIdType.MESH


def two_terms(values):
    values = np.asarray(values, np.float32)
    high = values.astype(jnp.bfloat16)
    low = (values - high.astype(np.float32)).astype(jnp.bfloat16)
    return high, low


def bit(value, index):
    return (value >> index) & 1


def owner_tables():
    row = np.arange(64)
    pick_one = np.zeros((64, 64), np.float32)
    pick_one[row, 8 * (row % 8) + row // 8] = 1
    row = np.arange(512)
    cell, coef, parent = row % 8, (row >> 4) & 7, 2 * (row >> 7) + bit(row, 3)
    pick_two = np.zeros((512, 64), np.float32)
    pick_two[row, 8 * cell + coef] = 1
    column = np.arange(512)
    source = np.where(column < 448, 8 + column // 8, (column - 448) // 8)
    spread_two = np.zeros((64, 512), np.float32)
    spread_two[source, column] = 1
    mask_two = (column[None, :] % 8 == parent[:, None]).astype(np.float32)
    row = np.arange(128)
    c2x, c3x, c2y, c3y, c1z, c2z, c3z = [bit(row, 6 - i) for i in range(7)]
    pick_three = np.zeros((128, 64), np.float32)
    pick_three[row, 8 * (4 * c3x + 2 * c3y + c3z)] = 1
    column = np.arange(1024)
    source = np.where(column < 896, 8 + column // 16, (column - 896) // 16)
    spread_three = np.zeros((64, 1024), np.float32)
    spread_three[source, column] = 1
    own = 8 * c1z + 4 * c2x + 2 * c2y + c2z
    mask_three = (column[None, :] % 16 == own[:, None]).astype(np.float32)
    picks = [pick_one, pick_two, spread_two, mask_two, pick_three, spread_three, mask_three]
    return [np.asarray(each, jnp.bfloat16) for each in picks]


def slot_tables():
    slot = np.arange(128)
    y_part = 2 * (slot // 32) + slot % 2
    z_part = (slot // 2) % 16
    mode = np.arange(128)
    kz, ky = mode // 8, mode % 8
    angle = 2 * np.pi * (np.outer(kz, z_part) / 16 + np.outer(ky, y_part) / 8)
    high, low = two_terms(np.concatenate([np.cos(angle), np.sin(angle)], axis=1))
    both = np.concatenate([high, low], axis=0)
    turn = 2 * np.pi * np.outer(np.arange(4), y_part) / 32
    turns = np.stack([np.cos(turn), np.sin(turn)]).astype(np.float32)
    return both, turns


def line_tables():
    z_low = np.arange(128)
    out = []
    for kz_low in range(16):
        angle = 2 * np.pi * np.outer(z_low, kz_low + 16 * np.arange(128)) / 2048
        cos, sin = np.cos(angle), np.sin(angle)
        out.append(np.block([[cos, -sin], [sin, cos]]))
    return np.stack(two_terms(np.stack(out)), axis=1)


def turn_tables():
    kt = np.arange(4)[:, None]
    s = np.arange(8)[None, :]
    ky_low = kt + 4 * s
    one = 2 * np.pi * ky_low[:, None, :] * np.arange(8)[None, :, None] / 256
    mode = ky_low[:, None, None, :] + 32 * np.arange(8)[None, None, :, None]
    two = 2 * np.pi * mode * np.arange(8)[None, :, None, None] / 2048
    wide = lambda a: np.ascontiguousarray(
        np.broadcast_to(np.stack([np.cos(a), np.sin(a)])[..., None], (2,) + a.shape + (128,))
    ).astype(np.float32)
    return wide(one), wide(two)


def digit_tables():
    out = []
    for pair in range(2):
        full = np.zeros((2, 2, 8, 8, 2, 2, 8, 8))
        for k in range(2):
            y2a = np.arange(8)[:, None]
            s = np.arange(8)[None, :]
            angle = 2 * np.pi * (s * y2a / 8 + (2 * pair + k) * y2a / 32)
            cos, sin = np.cos(angle), np.sin(angle)
            for y0 in range(8):
                full[0, k, :, y0, 0, k, y0, :] = cos
                full[0, k, :, y0, 1, k, y0, :] = -sin
                full[1, k, :, y0, 0, k, y0, :] = sin
                full[1, k, :, y0, 1, k, y0, :] = cos
        high, low = two_terms(full.reshape(256, 256))
        out.append(np.concatenate([high, low], axis=0))
    return np.stack(out)


def split(x):
    high = x.astype(BF16)
    return high, (x - high.astype(F32)).astype(BF16)


def dot(a, b):
    return jnp.dot(a, b, preferred_element_type=F32)


def dot_nt(a, b):
    return lax.dot_general(a, b, (((1,), (1,)), ((), ())), preferred_element_type=F32)


def add(a, b):
    return (a[0] + b[0], a[1] + b[1])


def sub(a, b):
    return (a[0] - b[0], a[1] - b[1])


def times(a, cos, sin, sign):
    if sign > 0:
        return (a[0] * cos - a[1] * sin, a[1] * cos + a[0] * sin)
    return (a[0] * cos + a[1] * sin, a[1] * cos - a[0] * sin)


def quarter(a, sign):
    return (-a[1], a[0]) if sign > 0 else (a[1], -a[0])


def add_quarter(a, b, sign):
    return (a[0] - b[1], a[1] + b[0]) if sign > 0 else (a[0] + b[1], a[1] - b[0])


def four(x, sign):
    even, odd = add(x[0], x[2]), add(x[1], x[3])
    left, right = sub(x[0], x[2]), sub(x[1], x[3])
    return [add(even, odd), add_quarter(left, right, sign), sub(even, odd),
            add_quarter(left, right, -sign)]


def eight(x, sign):
    even = four([x[0], x[2], x[4], x[6]], sign)
    odd = four([x[1], x[3], x[5], x[7]], sign)
    half = math.sqrt(0.5)
    a = odd[1]
    if sign > 0:
        odd1 = ((a[0] - a[1]) * half, (a[1] + a[0]) * half)
    else:
        odd1 = ((a[0] + a[1]) * half, (a[1] - a[0]) * half)
    a = odd[3]
    if sign > 0:
        odd3 = ((-a[0] - a[1]) * half, (a[0] - a[1]) * half)
    else:
        odd3 = ((a[1] - a[0]) * half, (-a[0] - a[1]) * half)
    return [
        add(even[0], odd[0]),
        add(even[1], odd1),
        add_quarter(even[2], odd[2], sign),
        add(even[3], odd3),
        sub(even[0], odd[0]),
        sub(even[1], odd1),
        add_quarter(even[2], odd[2], -sign),
        sub(even[3], odd3),
    ]


def sixteen(x, sign):
    out = [None] * 16
    mid = [four([x[a], x[a + 4], x[a + 8], x[a + 12]], sign) for a in range(4)]
    for c in range(4):
        terms = []
        for a in range(4):
            angle = 2 * math.pi * a * c / 16
            if a * c == 0:
                terms.append(mid[a][c])
            elif a * c == 4:
                terms.append(quarter(mid[a][c], sign))
            else:
                terms.append(times(mid[a][c], math.cos(angle), math.sin(angle), sign))
        done = four(terms, sign)
        for d in range(4):
            out[c + 4 * d] = done[d]
    return out


def prepare(mixing, picks, first_map, second_map, leaf_map):
    pick_one, pick_two, spread_two, mask_two, pick_three, spread_three, mask_three = picks
    mix = mixing[...]
    first_map[...] = dot(pick_one[...], mix).astype(BF16)
    rows = dot(pick_two[...], mix).astype(BF16)
    second_map[...] = (dot(rows, spread_two[...]) * mask_two[...].astype(F32)).astype(BF16)
    rows = dot(pick_three[...], mix).astype(BF16)
    leaf_map[...] = (dot(rows, spread_three[...]) * mask_three[...].astype(F32)).astype(BF16)


def expand(half, lanes, top, one, two, draws, arrived_draws, first_map, second_map, leaf_map,
           slots, turns, parents, leaves, high_rows, low_rows, sent):
    records = jnp.concatenate([top[:, lanes], one[:, lanes].astype(F32)], axis=0)
    high, low = split(records)
    high, low = split(dot(first_map[...], high) + dot(first_map[...], low))
    level_two = dot(second_map[...], jnp.concatenate([two[:, lanes], high], axis=0))
    low = jnp.concatenate([jnp.zeros_like(low), low], axis=0)
    level_two = level_two + dot(second_map[:, 384:], low)
    for tile in range(4):
        high, low = split(level_two[tile * 128:(tile + 1) * 128])
        parents[tile, 0:128] = high
        parents[tile, 128:256] = low

    @pl.loop(0, 2)
    def _(c1x):
        for c1y in range(2):
            tile = 2 * c1x + c1y
            arrived_draws(half, tile).wait()
            rows = pl.ds(pl.multiple_of(tile * 16, 16), 16)
            got = dot(leaf_map[:, :896], draws[half, :, rows, :].reshape(896, 512))
            near = parents[tile]
            got = got + dot(leaf_map[:, 896:], near[:128]) + dot(leaf_map[:, 896:], near[128:])
            for group in range(4):
                leaves[group, c1y] = got[group * 32:(group + 1) * 32]
        for pair in range(2):
            quarters = []
            for t in range(4):
                lane = t * 128
                re = leaves[2 * pair, :, :, lane:lane + 128].reshape(64, 128)
                im = leaves[2 * pair + 1, :, :, lane:lane + 128].reshape(64, 128)
                quarters.append((re, im))
            for k, value in enumerate(four(quarters, -1)):
                if k:
                    value = times(value, turns[0, k:k + 1], turns[1, k:k + 1], -1)
                re_high, re_low = split(value[0])
                im_high, im_low = split(value[1])
                base = pair * 128
                high_rows[k, base:base + 64, 0:128] = re_high
                high_rows[k, base:base + 64, 128:256] = im_high
                high_rows[k, base + 64:base + 128, 0:128] = im_high
                high_rows[k, base + 64:base + 128, 128:256] = -re_high
                low_rows[k, base:base + 64, 0:128] = re_low
                low_rows[k, base:base + 64, 128:256] = im_low
                low_rows[k, base + 64:base + 128, 0:128] = im_low
                low_rows[k, base + 64:base + 128, 128:256] = -re_low
        for k in range(4):
            both = dot_nt(slots[...], high_rows[k])
            done = both[:128] + both[128:] + dot_nt(slots[0:128], low_rows[k])
            for pair in range(2):
                piece = done[:, pair * 128:(pair + 1) * 128].reshape(16, 8, 128)
                sent[half, 2 * c1x + pair, :, k] = piece


def owner_index(q, w):
    index = 0
    for b in range(4):
        index += bit(w, b) << (2 * b)
    for b in range(3):
        index += bit(q, b) << (2 * b + 1)
    return index


def swap_lanes(x, lane):
    for b in range(4):
        width = 8 << b
        keep = (lane & width) == 0
        y = list(x)
        for i in range(16):
            if not bit(i, b):
                j = i | (1 << b)
                y[i] = jnp.where(keep, x[i], pltpu.roll(x[j], width, 1))
                y[j] = jnp.where(keep, pltpu.roll(x[i], 128 - width, 1), x[j])
        x = y
    return x


def along_lines(kt, arrived, factor, table, turn_one, turn_two, lane, flat, mid, work, spread):
    @pl.loop(0, 8)
    def _(q):
        base = 2 * (q % 2) + 8 * ((q // 2) % 2) + 32 * (q // 4)
        places = [owner_index(0, w) for w in range(16)]
        got = swap_lanes([arrived[base + place, kt] for place in places], lane)
        for oy in range(8):
            rows = pl.ds(pl.multiple_of(q * 64 + oy * 8, 8), 8)
            flat[rows, 0:128] = got[oy]
            flat[rows, 128:256] = got[8 + oy]

    for part in range(2):
        rows = pl.ds(part * 256, 256)
        high, low = split(flat[rows, :])
        mid[rows, :] = dot(high, table[0]) + dot(low, table[0]) + dot(high, table[1])

    @pl.loop(0, 8)
    def _(oy):
        x = []
        for q in range(8):
            rows = pl.ds(pl.multiple_of(q * 64 + oy * 8, 8), 8)
            value = (mid[rows, 0:128], mid[rows, 128:256])
            if q:
                value = times(value, turn_one[0, kt, q], turn_one[1, kt, q], -1)
            x.append(value)
        for k, value in enumerate(eight(x, -1)):
            value = times(value, turn_two[0, kt, oy, k], turn_two[1, kt, oy, k], -1)
            work[0, k, oy] = value[0]
            work[1, k, oy] = value[1]

    @pl.loop(0, 8)
    def _(kq):
        x = eight([(work[0, kq, oy], work[1, kq, oy]) for oy in range(8)], -1)
        y = []
        for k in range(8):
            rows = pl.ds(pl.multiple_of((kt * 8 + k) * 64 + kq * 8, 8), 8)
            scale = factor[rows, :]
            y.append((x[k][0] * scale, x[k][1] * scale))
        for y0, value in enumerate(eight(y, 1)):
            value = times(value, turn_two[0, kt, y0, kq], turn_two[1, kt, y0, kq], 1)
            work[0, kq, y0] = value[0]
            work[1, kq, y0] = value[1]

    @pl.loop(0, 8)
    def _(y0):
        x = [(work[0, kq, y0], work[1, kq, y0]) for kq in range(8)]
        for y1, value in enumerate(eight(x, 1)):
            if y1:
                value = times(value, turn_one[0, kt, y1], turn_one[1, kt, y1], 1)
            spread[0, kt, y1, y0] = value[0]
            spread[1, kt, y1, y0] = value[1]


def next_digit(ktp, digits, spread, mixed):
    @pl.loop(0, 4)
    def _(pair):
        columns = []
        for one in range(2):
            pieces = [
                spread[part, 2 * ktp + k, 2 * pair + one].reshape(64, 128)
                for part in range(2)
                for k in range(2)
            ]
            columns.append(jnp.concatenate(pieces, axis=0))
        high, low = split(jnp.concatenate(columns, axis=1))
        both = dot(digits[ktp], high)
        mixed[ktp, pair] = both[:256] + both[256:] + dot(digits[ktp, 0:256], low)


def last_digit(mixed, lined):
    @pl.loop(0, 4)
    def _(pair):
        for y2a in range(8):
            for one in range(2):
                x = []
                for kt in range(4):
                    base = (kt % 2) * 64 + y2a * 8
                    lanes = slice(one * 128, one * 128 + 128)
                    x.append((mixed[kt // 2, pair, base:base + 8, lanes],
                              mixed[kt // 2, pair, 128 + base:128 + base + 8, lanes]))
                for y2b, value in enumerate(four(x, 1)):
                    rows = pl.ds(pl.multiple_of((y2b * 8 + y2a) * 64 + (2 * pair + one) * 8, 8), 8)
                    lined[rows, 0:128] = value[0]
                    lined[rows, 128:256] = value[1]


PHASES = ((0, 3), (3, 1))


def whole_kernel(top, one, two, mixing, *refs):
    picks, refs = refs[:7], refs[7:]
    (slots, turns, digits, three, transfer, lines, turn_one_far, turn_two_far, out,
     first_map, second_map, leaf_map, draws, parents, leaves, high_rows, low_rows, sent, arrived,
     modes, factor, table, turn_one, turn_two, flat, mid, work, spread, mixed, lined, ready,
     draw_sem, fetch_sem, send_sem, recv_sem, back_send, back_recv) = refs
    row, col = lax.axis_index("row"), lax.axis_index("col")
    me = row * 16 + col
    core, z, y_low = lax.rem(col, 2), lax.rem(col // 2, 4), col // 8
    x, y_high = lax.rem(row, 4), row // 4

    barrier = pltpu.get_barrier_semaphore()

    @pl.loop(1, 128)
    def _(k):
        other = lax.rem(me + k, 128)
        pl.semaphore_signal(barrier, inc=1, device_id=(other // 16, lax.rem(other, 16)),
                            device_id_type=MESH)

    def lanes_of(half):
        e = lax.rem(half + core, 2)
        return pl.ds(pl.multiple_of(e * 512, 512), 512)

    def draw_copy(half, tile):
        rows = pl.ds(pl.multiple_of(tile * 16, 16), 16)
        return pltpu.make_async_copy(three.at[:, rows, lanes_of(half)],
                                     draws.at[half, :, rows, :], draw_sem.at[half, tile])

    for half in range(2):
        for tile in range(4):
            draw_copy(half, tile).start()
    fetches = [
        pltpu.make_async_copy(transfer, modes, fetch_sem.at[0]),
        pltpu.make_async_copy(lines.at[col], table, fetch_sem.at[1]),
        pltpu.make_async_copy(turn_one_far, turn_one, fetch_sem.at[2]),
        pltpu.make_async_copy(turn_two_far, turn_two, fetch_sem.at[3]),
    ]
    for fetch in fetches:
        fetch.start()
    prepare(mixing, picks, first_map, second_map, leaf_map)

    def send(half, phase):
        first, count = PHASES[phase]
        kts = pl.ds(first, count)
        e = lax.rem(half + core, 2)

        @pl.loop(0, 64)
        def _(k):
            j = lax.rem(k * 37 + 37, 64)
            to_x = lax.rem(x + lax.rem(j, 4), 4)
            to_z = lax.rem(z + lax.rem(j // 4, 4), 4)
            to_y = lax.rem(y_low + lax.rem(j // 16, 2), 2)
            to_core = lax.rem(core + j // 32, 2)
            to_row, to_col = 4 * e + to_x, to_y * 8 + to_z * 2 + to_core
            here = jnp.logical_and(to_row == row, to_col == col)

            @pl.when(jnp.logical_not(here))
            def _():
                pltpu.make_async_remote_copy(
                    sent.at[half, to_x, to_col, kts], arrived.at[me, kts],
                    send_sem.at[half, phase], recv_sem.at[phase],
                    device_id=(to_row, to_col), device_id_type=MESH).start()

            @pl.when(here)
            def _():
                pltpu.make_async_copy(sent.at[half, to_x, to_col, kts], arrived.at[me, kts],
                                      send_sem.at[half, phase]).start()

    def sent_all(half, phase):
        first, count = PHASES[phase]
        view = sent.at[half, :, :, pl.ds(first, count)]
        pltpu.make_async_copy(view, view, send_sem.at[half, phase]).wait()

    def received_all(phase):
        first, count = PHASES[phase]
        view = arrived.at[pl.ds(0, 127), pl.ds(first, count)]
        pltpu.make_async_copy(view, view, recv_sem.at[phase]).wait()

    for half in range(2):
        expand(half, lanes_of(half), top, one, two, draws, draw_copy, first_map, second_map,
               leaf_map, slots, turns, parents, leaves, high_rows, low_rows, sent)
        if half == 0:
            pl.semaphore_wait(barrier, 127)
        send(half, 0)

    for fetch in fetches:
        fetch.wait()

    @pl.loop(0, 128)
    def _(i):
        low, kt, high = i // 32, lax.rem(i // 8, 4), lax.rem(i, 8)
        rows = modes[pl.ds(pl.multiple_of((low * 4 + kt) * 128 + high * 16, 16), 16), :]
        factor[pl.ds((kt * 8 + high) * 64 + low, 16, stride=4), :] = rows * (1.0 / (2048 * 2048))

    sent_all(0, 0)
    send(0, 1)
    sent_all(1, 0)
    send(1, 1)

    lane = lax.broadcasted_iota(jnp.int32, (8, 128), 1)
    for phase in range(2):
        if phase:
            sent_all(0, 1)
            sent_all(1, 1)
        received_all(phase)
        first, count = PHASES[phase]

        @pl.loop(first, first + count)
        def _(kt):
            along_lines(kt, arrived, factor, table, turn_one, turn_two, lane, flat, mid, work,
                        spread)

        next_digit(phase, digits, spread, mixed)

    last_digit(mixed, lined)

    @pl.loop(0, 16)
    def _(k):
        j = lax.rem(k * 7 + 7, 16)
        to_z = lax.rem(z + lax.rem(j // 2, 4), 4)
        to_y = lax.rem(y_low + lax.rem(j, 2), 2)
        to_core = lax.rem(core + j // 8, 2)
        to = to_y * 8 + to_z * 2 + to_core
        high, low = split(lined[pl.ds(pl.multiple_of(to * 128, 128), 128), :])
        both = dot_nt(jnp.concatenate([high, low], axis=0), table[0])
        done = both[:128] + both[128:] + dot_nt(high, table[1])
        ready[to, 0] = done[:, :128]
        ready[to, 1] = done[:, 128:]

        @pl.when(to != col)
        def _():
            pltpu.make_async_remote_copy(ready.at[to], out.at[col], back_send, back_recv,
                                         device_id=(row, to), device_id_type=MESH).start()

        @pl.when(to == col)
        def _():
            pltpu.make_async_copy(ready.at[to], out.at[col], back_send).start()

    pltpu.make_async_copy(ready, ready, back_send).wait()
    view = ready.at[pl.ds(0, 15)]
    pltpu.make_async_copy(view, view, back_recv).wait()


def whole(top, one, two, three, mixing, transfer):
    slots, turns = slot_tables()
    turn_one, turn_two = turn_tables()
    near = [top, one, two.reshape(448, 1024), mixing] + owner_tables()
    near += [slots, turns, digit_tables()]
    far = [three, transfer, line_tables(), turn_one, turn_two]
    inside, outside = pl.BlockSpec(memory_space=VMEM), pl.BlockSpec(memory_space=pl.ANY)
    dma = pltpu.SemaphoreType.DMA
    return pl.pallas_call(
        whole_kernel,
        in_specs=[inside] * len(near) + [outside] * len(far),
        out_specs=outside,
        out_shape=jax.ShapeDtypeStruct((16, 2, 128, 128), F32),
        scratch_shapes=[
            VMEM((64, 64), BF16),
            VMEM((512, 512), BF16),
            VMEM((128, 1024), BF16),
            VMEM((2, 56, 64, 512), BF16),
            VMEM((4, 256, 512), BF16),
            VMEM((4, 2, 32, 512), F32),
            VMEM((4, 256, 256), BF16),
            VMEM((4, 256, 256), BF16),
            VMEM((2, 4, 16, 4, 8, 128), F32),
            VMEM((128, 4, 8, 128), F32),
            VMEM((2048, 128), F32),
            VMEM((2048, 128), F32),
            VMEM((2, 256, 256), BF16),
            VMEM((2, 4, 8, 8, 128), F32),
            VMEM((2, 4, 8, 8, 8, 128), F32),
            VMEM((512, 256), F32),
            VMEM((512, 256), F32),
            VMEM((2, 8, 8, 8, 128), F32),
            VMEM((2, 4, 8, 8, 8, 128), F32),
            VMEM((2, 4, 256, 256), F32),
            VMEM((2048, 256), F32),
            VMEM((16, 2, 128, 128), F32),
            dma((2, 4)),
            dma((4,)),
            dma((2, 2)),
            dma((2,)),
            dma,
            dma,
        ],
        compiler_params=pltpu.CompilerParams(
            collective_id=0, has_side_effects=True, vmem_limit_bytes=56 * 2**20),
    )(*[jnp.asarray(a) for a in near + far])


def strip_kernel(arrived, out):
    @pl.loop(0, 4)
    def _(tile):
        rows = pl.ds(pl.multiple_of(tile * 8, 8), 8)
        x = [(arrived[k, 0, rows, :], arrived[k, 1, rows, :]) for k in range(16)]
        for z, value in enumerate(sixteen(x, 1)):
            out[0, rows, z * 128:(z + 1) * 128] = value[0]
            out[1, rows, z * 128:(z + 1) * 128] = value[1]


def strips(arrived):
    return pl.pallas_call(
        strip_kernel,
        grid=(4,),
        in_specs=[pl.BlockSpec((16, 2, 32, 128), lambda i: (0, 0, i, 0))],
        out_specs=pl.BlockSpec((2, 32, 2048), lambda i: (0, i, 0)),
        out_shape=jax.ShapeDtypeStruct((2, 128, 2048), F32),
        compiler_params=pltpu.CompilerParams(vmem_limit_bytes=32 * 2**20),
    )(arrived)


def body(top, one, two, three, mixing, transfer):
    return strips(whole(top, one, two, three, mixing, transfer))


def solution(mesh):
    return jax.shard_map(
        body,
        mesh=mesh,
        in_specs=(
            P(None, ("row", "col")),
            P(None, ("row", "col")),
            P(None, None, ("row", "col")),
            P(None, None, ("row", "col")),
            P(),
            P(None, "col"),
        ),
        out_specs=P("row", "col", None),
        check_vma=False,
    )
```

```python
import math

import jax
import jax.numpy as jnp
import numpy as np
from jax import lax
from jax.experimental import pallas as pl
from jax.experimental.pallas import tpu as pltpu
from jax.sharding import PartitionSpec as P

F32 = jnp.float32
BF16 = jnp.bfloat16
VMEM = pltpu.VMEM
MESH = pl.DeviceIdType.MESH


def two_terms(values):
    values = np.asarray(values, np.float32)
    high = values.astype(jnp.bfloat16)
    low = (values - high.astype(np.float32)).astype(jnp.bfloat16)
    return high, low


def bit(value, index):
    return (value >> index) & 1


def owner_tables():
    row = np.arange(64)
    pick_one = np.zeros((64, 64), np.float32)
    pick_one[row, 8 * (row % 8) + row // 8] = 1
    row = np.arange(512)
    pick_two = np.zeros((512, 64), np.float32)
    pick_two[row, 8 * (row % 8) + ((row >> 4) & 7)] = 1
    row = np.arange(128)
    pick_three = np.zeros((128, 64), np.float32)
    pick_three[row, 8 * (4 * bit(row, 5) + 2 * bit(row, 3) + bit(row, 0))] = 1
    return [np.asarray(each, jnp.bfloat16) for each in (pick_one, pick_two, pick_three)]


def slot_tables():
    slot = np.arange(128)
    y_part = 2 * (slot // 32) + slot % 2
    z_part = (slot // 2) % 16
    mode = np.arange(128)
    kz, ky = mode // 8, mode % 8
    angle = np.outer(kz, z_part) / 16 + np.outer(ky, y_part) / 8
    angle = 2 * np.pi * (angle[None] + kz[None, :, None] * np.arange(16)[:, None, None] / 256)
    high, low = two_terms(np.concatenate([np.cos(angle), np.sin(angle)], axis=2))
    both = np.concatenate([high, low], axis=1)
    turn = 2 * np.pi * np.outer(np.arange(4), y_part) / 32
    turns = np.stack([np.cos(turn), np.sin(turn)]).astype(np.float32)
    return both, turns


def line_tables():
    z_low, kz_high = np.arange(128), np.arange(128)
    sign = 1 - 2 * (kz_high % 2)
    ahead, back = [], []
    for kz_low in range(16):
        angle = 2 * np.pi * np.outer(z_low, kz_low + 16 * kz_high) / 2048
        cos, sin = np.cos(angle), np.sin(angle)
        back.append(np.block([[cos, -sin], [sin, cos]]))
        angle = np.outer(z_low, kz_high) / 128 + (z_low % 8)[:, None] * kz_low / 2048
        cos, sin = np.cos(2 * np.pi * angle), np.sin(2 * np.pi * angle)
        ahead.append(np.block([[cos, -sin], [sin * sign, cos * sign]]))
    pair = lambda a: np.stack(two_terms(np.stack(a)), axis=1)
    return pair(ahead), pair(back)


def turn_tables():
    kt = np.arange(4)[:, None]
    s = np.arange(8)[None, :]
    ky_low = kt + 4 * s
    one = 2 * np.pi * ky_low[:, None, :] * np.arange(8)[None, :, None] / 256
    mode = ky_low[:, None, None, :] + 32 * np.arange(8)[None, None, :, None]
    two = 2 * np.pi * mode * np.arange(8)[None, :, None, None] / 2048
    wide = lambda a: np.ascontiguousarray(
        np.broadcast_to(np.stack([np.cos(a), np.sin(a)])[..., None], (2,) + a.shape + (128,))
    ).astype(np.float32)
    moved = two[..., None] - 2 * np.pi * np.multiply.outer(np.arange(8), np.arange(128))[
        None, :, None, None, :] / 16
    moved = np.stack([np.cos(moved), np.sin(moved)]).astype(np.float32)
    return wide(one), wide(two), moved


def digit_tables():
    out = []
    for pair in range(2):
        full = np.zeros((2, 2, 8, 8, 2, 2, 8, 8))
        for k in range(2):
            y2a = np.arange(8)[:, None]
            s = np.arange(8)[None, :]
            angle = 2 * np.pi * (s * y2a / 8 + (2 * pair + k) * y2a / 32)
            cos, sin = np.cos(angle), np.sin(angle)
            for y0 in range(8):
                full[0, k, :, y0, 0, k, y0, :] = cos
                full[0, k, :, y0, 1, k, y0, :] = -sin
                full[1, k, :, y0, 0, k, y0, :] = sin
                full[1, k, :, y0, 1, k, y0, :] = cos
        high, low = two_terms(full.reshape(256, 256))
        out.append(np.concatenate([high, low], axis=0))
    return np.stack(out)


def split(x):
    high = x.astype(BF16)
    return high, (x - high.astype(F32)).astype(BF16)


def dot(a, b):
    return jnp.dot(a, b, preferred_element_type=F32)


def dot_nt(a, b):
    return lax.dot_general(a, b, (((1,), (1,)), ((), ())), preferred_element_type=F32)


def add(a, b):
    return (a[0] + b[0], a[1] + b[1])


def sub(a, b):
    return (a[0] - b[0], a[1] - b[1])


def times(a, cos, sin, sign):
    if sign > 0:
        return (a[0] * cos - a[1] * sin, a[1] * cos + a[0] * sin)
    return (a[0] * cos + a[1] * sin, a[1] * cos - a[0] * sin)


def quarter(a, sign):
    return (-a[1], a[0]) if sign > 0 else (a[1], -a[0])


def add_quarter(a, b, sign):
    return (a[0] - b[1], a[1] + b[0]) if sign > 0 else (a[0] + b[1], a[1] - b[0])


def four(x, sign):
    even, odd = add(x[0], x[2]), add(x[1], x[3])
    left, right = sub(x[0], x[2]), sub(x[1], x[3])
    return [add(even, odd), add_quarter(left, right, sign), sub(even, odd),
            add_quarter(left, right, -sign)]


def eight(x, sign):
    even = four([x[0], x[2], x[4], x[6]], sign)
    odd = four([x[1], x[3], x[5], x[7]], sign)
    half = math.sqrt(0.5)
    a = odd[1]
    if sign > 0:
        odd1 = ((a[0] - a[1]) * half, (a[1] + a[0]) * half)
    else:
        odd1 = ((a[0] + a[1]) * half, (a[1] - a[0]) * half)
    a = odd[3]
    if sign > 0:
        odd3 = ((-a[0] - a[1]) * half, (a[0] - a[1]) * half)
    else:
        odd3 = ((a[1] - a[0]) * half, (-a[0] - a[1]) * half)
    return [
        add(even[0], odd[0]),
        add(even[1], odd1),
        add_quarter(even[2], odd[2], sign),
        add(even[3], odd3),
        sub(even[0], odd[0]),
        sub(even[1], odd1),
        add_quarter(even[2], odd[2], -sign),
        sub(even[3], odd3),
    ]


def sixteen(x, sign):
    out = [None] * 16
    mid = [four([x[a], x[a + 4], x[a + 8], x[a + 12]], sign) for a in range(4)]
    for c in range(4):
        terms = []
        for a in range(4):
            angle = 2 * math.pi * a * c / 16
            if a * c == 0:
                terms.append(mid[a][c])
            elif a * c == 4:
                terms.append(quarter(mid[a][c], sign))
            else:
                terms.append(times(mid[a][c], math.cos(angle), math.sin(angle), sign))
        done = four(terms, sign)
        for d in range(4):
            out[c + 4 * d] = done[d]
    return out


def spread(rows, width, own):
    shape = (64, 64 * width)
    column = lax.broadcasted_iota(jnp.int32, shape, 1) // width
    source = lax.broadcasted_iota(jnp.int32, shape, 0)
    wide = dot(rows.astype(BF16), (((column + 8) & 63) == source).astype(F32).astype(BF16))
    shape = (rows.shape[0], 64 * width)
    cell = lax.broadcasted_iota(jnp.int32, shape, 1) & (width - 1)
    return jnp.where(cell == own(lax.broadcasted_iota(jnp.int32, shape, 0)), wide, 0.0).astype(BF16)


def prepare(mixing, picks, first_map, second_map, leaf_map):
    mix = mixing[...]
    first_map[...] = dot(picks[0][...], mix).astype(BF16)
    second_map[...] = spread(dot(picks[1][...], mix), 8, lambda r: 2 * (r >> 7) + bit(r, 3))
    leaf_map[...] = spread(
        dot(picks[2][...], mix), 16,
        lambda r: 8 * bit(r, 2) + 4 * bit(r, 6) + 2 * bit(r, 4) + bit(r, 1))


def expand(half, digit, lanes, top, one, two, draws, arrived_draws, first_map, second_map, leaf_map,
           slots, turns, parents, leaves, high_rows, low_rows, sent):
    records = jnp.concatenate([top[:, lanes], one[:, lanes].astype(F32)], axis=0)
    high, low = split(records)
    high, low = split(dot(first_map[...], high) + dot(first_map[...], low))
    level_two = dot(second_map[...], jnp.concatenate([two[half], high], axis=0))
    low = jnp.concatenate([jnp.zeros_like(low), low], axis=0)
    level_two = level_two + dot(second_map[:, 384:], low)
    for tile in range(4):
        high, low = split(level_two[tile * 128:(tile + 1) * 128])
        parents[tile, 0:128] = high
        parents[tile, 128:256] = low

    @pl.loop(0, 2)
    def _(c1x):
        for c1y in range(2):
            tile = 2 * c1x + c1y
            arrived_draws(half, tile).wait()
            rows = pl.ds(pl.multiple_of(tile * 16, 16), 16)
            got = dot(leaf_map[:, :896], draws[half, :, rows, :].reshape(896, 512))
            near = parents[tile]
            got = got + dot(leaf_map[:, 896:], near[:128]) + dot(leaf_map[:, 896:], near[128:])
            for group in range(4):
                for i in range(4):
                    row = group * 32 + i * 8
                    leaves[group // 2, group % 2, 4 * c1y + i] = got[row:row + 8]

        @pl.loop(0, 8)
        def _(twin):
            for pair in range(2):
                quarters = []
                for t in range(4):
                    lane = slice(t * 128, t * 128 + 128)
                    first, second = [], []
                    for j in range(2):
                        group = lax.rem(2 * twin + j - digit + 16, 16)
                        part, oy = group // 8, lax.rem(group, 8)
                        first.append(leaves[pair, part, oy, :, lane])
                        other = leaves[pair, 1 - part, oy, :, lane]
                        second.append(other * (1 - 2 * part).astype(F32))
                    quarters.append((jnp.concatenate(first, axis=0), jnp.concatenate(second, axis=0)))
                rows = pl.ds(pl.multiple_of(pair * 128 + twin * 16, 16), 16)
                for k, value in enumerate(four(quarters, -1)):
                    if k:
                        value = times(value, turns[0, k:k + 1], turns[1, k:k + 1], -1)
                    for side in range(2):
                        high, low = split(value[side])
                        high_rows[k, rows, side * 128:side * 128 + 128] = high
                        low_rows[k, rows, side * 128:side * 128 + 128] = low

        for k in range(4):
            both = dot_nt(slots[...], high_rows[k])
            done = both[:128] + both[128:] + dot_nt(slots[0:128], low_rows[k])
            for pair in range(2):
                piece = done[:, pair * 128:(pair + 1) * 128].reshape(16, 8, 128)
                sent[half, 2 * c1x + pair, :, k] = piece


def owner_index(q, w):
    index = 0
    for b in range(4):
        index += bit(w, b) << (2 * b)
    for b in range(3):
        index += bit(q, b) << (2 * b + 1)
    return index


def gather_lanes(x, lane):
    for b in range(4):
        here = (lane & (8 << b)) != 0
        x = [jnp.where(here, x[(m + (1 << b)) % 16], x[m]) for m in range(16)]
    return [x[(16 - d) % 16] for d in range(16)]


def along_lines(kt, arrived, factor, table, turn_one, turn_two, moved, lane, flat, mid, work, placed):
    @pl.loop(0, 8, unroll=2)
    def _(q):
        base = 2 * (q % 2) + 8 * ((q // 2) % 2) + 32 * (q // 4)
        places = [owner_index(0, w) for w in range(16)]
        got = gather_lanes([arrived[base + place, kt] for place in places], lane)
        for oy in range(8):
            rows = pl.ds(pl.multiple_of(q * 64 + oy * 8, 8), 8)
            flat[rows, 0:128] = got[oy]
            flat[rows, 128:256] = got[8 + oy]

    for part in range(2):
        rows = pl.ds(part * 256, 256)
        high, low = split(flat[rows, :])
        mid[rows, :] = dot(high, table[0]) + dot(low, table[0]) + dot(high, table[1])

    @pl.loop(0, 8, unroll=2)
    def _(oy):
        x = []
        for q in range(8):
            rows = pl.ds(pl.multiple_of(q * 64 + oy * 8, 8), 8)
            value = (mid[rows, 0:128], mid[rows, 128:256])
            if q:
                value = times(value, turn_one[0, kt, q], turn_one[1, kt, q], -1)
            x.append(value)
        for k, value in enumerate(eight(x, -1)):
            value = times(value, moved[0, kt, oy, k], moved[1, kt, oy, k], -1)
            work[0, k, oy] = value[0]
            work[1, k, oy] = value[1]

    @pl.loop(0, 8, unroll=2)
    def _(kq):
        x = eight([(work[0, kq, oy], work[1, kq, oy]) for oy in range(8)], -1)
        y = []
        for k in range(8):
            rows = pl.ds(pl.multiple_of((kt * 8 + k) * 64 + kq * 8, 8), 8)
            scale = factor[rows, :]
            y.append((x[k][0] * scale, x[k][1] * scale))
        for y0, value in enumerate(eight(y, 1)):
            value = times(value, turn_two[0, kt, y0, kq], turn_two[1, kt, y0, kq], 1)
            work[0, kq, y0] = value[0]
            work[1, kq, y0] = value[1]

    @pl.loop(0, 8, unroll=2)
    def _(y0):
        x = [(work[0, kq, y0], work[1, kq, y0]) for kq in range(8)]
        for y1, value in enumerate(eight(x, 1)):
            if y1:
                value = times(value, turn_one[0, kt, y1], turn_one[1, kt, y1], 1)
            placed[0, kt, y1, y0] = value[0]
            placed[1, kt, y1, y0] = value[1]


def next_digit(ktp, digits, placed, mixed):
    @pl.loop(0, 4, unroll=True)
    def _(pair):
        columns = []
        for one in range(2):
            pieces = [
                placed[part, 2 * ktp + k, 2 * pair + one].reshape(64, 128)
                for part in range(2)
                for k in range(2)
            ]
            columns.append(jnp.concatenate(pieces, axis=0))
        high, low = split(jnp.concatenate(columns, axis=1))
        both = dot(digits[ktp], high)
        mixed[ktp, pair] = both[:256] + both[256:] + dot(digits[ktp, 0:256], low)


def last_digit(odd, mixed, lined):
    @pl.loop(0, 4, unroll=True)
    def _(pair):
        for y2a in range(odd, 8, 2):
            for one in range(2):
                x = []
                for kt in range(4):
                    base = (kt % 2) * 64 + y2a * 8
                    lanes = slice(one * 128, one * 128 + 128)
                    x.append((mixed[kt // 2, pair, base:base + 8, lanes],
                              mixed[kt // 2, pair, 128 + base:128 + base + 8, lanes]))
                for y2b, value in enumerate(four(x, 1)):
                    rows = pl.ds(pl.multiple_of((y2b * 8 + y2a) * 64 + (2 * pair + one) * 8, 8), 8)
                    lined[rows, 0:128] = value[0]
                    lined[rows, 128:256] = value[1]


PHASES = ((0, 3), (3, 1))


def whole_kernel(top, one, mixing, *refs):
    picks, refs = refs[:3], refs[3:]
    (turns, three, two_far, digits_far, slots_far, transfer, ahead_far, back_far, turn_one_far, turn_two_far,
     moved_far, out,
     first_map, second_map, leaf_map, two, digits, draws, parents, leaves, high_rows, low_rows, sent, arrived,
     slots, modes, factor, ahead, back, turn_one, turn_two, moved, flat, mid, work, placed, mixed, lined, ready,
     landed, strip,     draw_sem, fetch_sem, send_sem, recv_sem, back_send, back_recv,
     out_sem, two_sem) = refs
    row, col = lax.axis_index("row"), lax.axis_index("col")
    me = row * 16 + col
    core, z, y_low = lax.rem(col, 2), lax.rem(col // 2, 4), col // 8
    x, y_high = lax.rem(row, 4), row // 4

    digit = (lax.rem(col, 2) + 2 * lax.rem(col // 4, 2) + 4 * lax.rem(row, 2)
             + 8 * lax.rem(row // 4, 2))

    barrier = pltpu.get_barrier_semaphore()

    @pl.loop(1, 128)
    def _(k):
        other = lax.rem(me + k, 128)
        pl.semaphore_signal(barrier, inc=1, device_id=(other // 16, lax.rem(other, 16)),
                            device_id_type=MESH)

    def lanes_of(half):
        e = lax.rem(half + core, 2)
        return pl.ds(pl.multiple_of(e * 512, 512), 512)

    def draw_copy(half, tile):
        rows = pl.ds(pl.multiple_of(tile * 16, 16), 16)
        return pltpu.make_async_copy(three.at[:, rows, lanes_of(half)],
                                     draws.at[half, :, rows, :], draw_sem.at[half, tile])

    fetch_slots = pltpu.make_async_copy(slots_far.at[digit], slots, fetch_sem.at[6])
    fetch_slots.start()
    def two_copy(half):
        return pltpu.make_async_copy(two_far.at[:, lanes_of(half)], two.at[half], two_sem.at[half])

    for half in range(2):
        two_copy(half).start()
        for tile in range(4):
            draw_copy(half, tile).start()
    fetches = [
        pltpu.make_async_copy(transfer, modes, fetch_sem.at[0]),
        pltpu.make_async_copy(ahead_far.at[col], ahead, fetch_sem.at[1]),
        pltpu.make_async_copy(back_far.at[col], back, fetch_sem.at[4]),
        pltpu.make_async_copy(moved_far, moved, fetch_sem.at[5]),
        pltpu.make_async_copy(digits_far, digits, fetch_sem.at[7]),
        pltpu.make_async_copy(turn_one_far, turn_one, fetch_sem.at[2]),
        pltpu.make_async_copy(turn_two_far, turn_two, fetch_sem.at[3]),
    ]
    prepare(mixing, picks, first_map, second_map, leaf_map)
    fetch_slots.wait()

    def send(half, phase):
        first, count = PHASES[phase]
        kts = pl.ds(first, count)
        e = lax.rem(half + core, 2)

        @pl.loop(0, 64)
        def _(k):
            j = lax.rem(k * 37 + 37, 64)
            to_x = lax.rem(x + lax.rem(j, 4), 4)
            to_z = lax.rem(z + lax.rem(j // 4, 4), 4)
            to_y = lax.rem(y_low + lax.rem(j // 16, 2), 2)
            to_core = lax.rem(core + j // 32, 2)
            to_row, to_col = 4 * e + to_x, to_y * 8 + to_z * 2 + to_core
            here = jnp.logical_and(to_row == row, to_col == col)

            @pl.when(jnp.logical_not(here))
            def _():
                pltpu.make_async_remote_copy(
                    sent.at[half, to_x, to_col, kts], arrived.at[me, kts],
                    send_sem.at[half, phase], recv_sem.at[phase],
                    device_id=(to_row, to_col), device_id_type=MESH).start()

            @pl.when(here)
            def _():
                pltpu.make_async_copy(sent.at[half, to_x, to_col, kts], arrived.at[me, kts],
                                      send_sem.at[half, phase]).start()

    def sent_all(half, phase):
        first, count = PHASES[phase]
        view = sent.at[half, :, :, pl.ds(first, count)]
        pltpu.make_async_copy(view, view, send_sem.at[half, phase]).wait()

    def received_all(phase):
        first, count = PHASES[phase]
        view = arrived.at[pl.ds(0, 127), pl.ds(first, count)]
        pltpu.make_async_copy(view, view, recv_sem.at[phase]).wait()

    for half in range(2):
        two_copy(half).wait()
        expand(half, digit, lanes_of(half), top, one, two, draws, draw_copy, first_map, second_map,
               leaf_map, slots, turns, parents, leaves, high_rows, low_rows, sent)
        if half == 0:
            pl.semaphore_wait(barrier, 127)
        send(half, 0)
        if half == 0:
            for fetch in fetches:
                fetch.start()

    for fetch in fetches:
        fetch.wait()

    @pl.loop(0, 128)
    def _(i):
        low, kt, high = i // 32, lax.rem(i // 8, 4), lax.rem(i, 8)
        rows = modes[pl.ds(pl.multiple_of((low * 4 + kt) * 128 + high * 16, 16), 16), :]
        factor[pl.ds((kt * 8 + high) * 64 + low, 16, stride=4), :] = rows * (1.0 / (2048 * 2048))

    sent_all(0, 0)
    send(0, 1)
    sent_all(1, 0)
    send(1, 1)

    lane = lax.broadcasted_iota(jnp.int32, (8, 128), 1)
    for phase in range(2):
        if phase:
            sent_all(0, 1)
            sent_all(1, 1)
        received_all(phase)
        first, count = PHASES[phase]

        @pl.loop(first, first + count)
        def _(kt):
            along_lines(kt, arrived, factor, ahead, turn_one, turn_two, moved, lane, flat, mid, work,
                        placed)

        next_digit(phase, digits, placed, mixed)

    for odd in range(2):
        last_digit(odd, mixed, lined)
        half_strip = pl.ds(odd * 64, 64)

        @pl.loop(0, 16)
        def _(k):
            j = lax.rem(k * 7 + 7, 16)
            to_z = lax.rem(z + lax.rem(j // 2, 4), 4)
            to_y = lax.rem(y_low + lax.rem(j, 2), 2)
            to_core = lax.rem(core + j // 8, 2)
            to = to_y * 8 + to_z * 2 + to_core
            rows = pl.ds(pl.multiple_of(to * 128 + odd * 64, 64), 64)
            high, low = split(lined[rows, :])
            both = dot_nt(jnp.concatenate([high, low], axis=0), back[0])
            done = both[:64] + both[64:] + dot_nt(high, back[1])
            ready[to, 0, half_strip, :] = done[:, :128]
            ready[to, 1, half_strip, :] = done[:, 128:]
            source = ready.at[to, :, half_strip, :]
            target = landed.at[col, :, half_strip, :]

            @pl.when(to != col)
            def _():
                pltpu.make_async_remote_copy(
                    source, target, back_send.at[odd], back_recv.at[odd],
                    device_id=(row, to), device_id_type=MESH).start()

            @pl.when(to == col)
            def _():
                pltpu.make_async_copy(source, target, back_send.at[odd]).start()

    for odd in range(2):
        half_strip = pl.ds(odd * 64, 64)
        view = ready.at[:, :, half_strip, :]
        pltpu.make_async_copy(view, view, back_send.at[odd]).wait()
        view = ready.at[pl.ds(0, 15), :, half_strip, :]
        pltpu.make_async_copy(view, view, back_recv.at[odd]).wait()

        @pl.loop(0, 8)
        def _(tile):
            rows = pl.ds(pl.multiple_of(odd * 64 + tile * 8, 8), 8)
            x = [(landed[k, 0, rows, :], landed[k, 1, rows, :]) for k in range(16)]
            for place, value in enumerate(sixteen(x, 1)):
                strip[0, rows, place * 128:(place + 1) * 128] = value[0]
                strip[1, rows, place * 128:(place + 1) * 128] = value[1]

        pltpu.make_async_copy(strip.at[:, half_strip, :], out.at[:, half_strip, :],
                              out_sem.at[odd]).start()
    for odd in range(2):
        half_strip = pl.ds(odd * 64, 64)
        pltpu.make_async_copy(strip.at[:, half_strip, :], out.at[:, half_strip, :],
                              out_sem.at[odd]).wait()


def whole(top, one, two, three, mixing, transfer):
    slots, turns = slot_tables()
    turn_one, turn_two, moved = turn_tables()
    ahead, back = line_tables()
    near = [top, one, mixing] + owner_tables()
    near += [turns]
    far = [three, two.reshape(448, 1024), digit_tables(), slots, transfer, ahead, back, turn_one, turn_two, moved]
    inside, outside = pl.BlockSpec(memory_space=VMEM), pl.BlockSpec(memory_space=pl.ANY)
    dma = pltpu.SemaphoreType.DMA
    return pl.pallas_call(
        whole_kernel,
        in_specs=[inside] * len(near) + [outside] * len(far),
        out_specs=outside,
        out_shape=jax.ShapeDtypeStruct((2, 128, 2048), F32),
        scratch_shapes=[
            VMEM((64, 64), BF16),
            VMEM((512, 512), BF16),
            VMEM((128, 1024), BF16),
            VMEM((2, 448, 512), BF16),
            VMEM((2, 512, 256), BF16),
            VMEM((2, 56, 64, 512), BF16),
            VMEM((4, 256, 512), BF16),
            VMEM((2, 2, 8, 8, 512), F32),
            VMEM((4, 256, 256), BF16),
            VMEM((4, 256, 256), BF16),
            VMEM((2, 4, 16, 4, 8, 128), F32),
            VMEM((128, 4, 8, 128), F32),
            VMEM((256, 256), BF16),
            VMEM((2048, 128), F32),
            VMEM((2056, 128), F32),
            VMEM((2, 256, 256), BF16),
            VMEM((2, 256, 256), BF16),
            VMEM((2, 4, 8, 8, 128), F32),
            VMEM((2, 4, 8, 8, 8, 128), F32),
            VMEM((2, 4, 8, 8, 8, 128), F32),
            VMEM((512, 256), F32),
            VMEM((512, 256), F32),
            VMEM((2, 8, 8, 8, 128), F32),
            VMEM((2, 4, 8, 8, 8, 128), F32),
            VMEM((2, 4, 256, 256), F32),
            VMEM((2048, 256), F32),
            VMEM((16, 2, 128, 128), F32),
            VMEM((16, 2, 128, 128), F32),
            VMEM((2, 128, 2048), F32),
            dma((2, 4)),
            dma((8,)),
            dma((2, 2)),
            dma((2,)),
            dma((2,)),
            dma((2,)),
            dma((2,)),
            dma((2,)),
        ],
        compiler_params=pltpu.CompilerParams(
            collective_id=0, has_side_effects=True, vmem_limit_bytes=56 * 2**20),
    )(*[jnp.asarray(a) for a in near + far])


def solution(mesh):
    return jax.shard_map(
        whole,
        mesh=mesh,
        in_specs=(
            P(None, ("row", "col")),
            P(None, ("row", "col")),
            P(None, None, ("row", "col")),
            P(None, None, ("row", "col")),
            P(),
            P(None, "col"),
        ),
        out_specs=P("row", "col", None),
        check_vma=False,
    )
```

```python
import math

import jax
import jax.numpy as jnp
import numpy as np
from jax import lax
from jax.experimental import pallas as pl
from jax.experimental.pallas import tpu as pltpu
from jax.sharding import PartitionSpec as P

F32 = jnp.float32
BF16 = jnp.bfloat16
VMEM = pltpu.VMEM
MESH = pl.DeviceIdType.MESH


def two_terms(values):
    values = np.asarray(values, np.float32)
    high = values.astype(jnp.bfloat16)
    low = (values - high.astype(np.float32)).astype(jnp.bfloat16)
    return high, low


def bit(value, index):
    return (value >> index) & 1


def owner_tables():
    row = np.arange(64)
    pick_one = np.zeros((64, 64), np.float32)
    pick_one[row, 8 * (row % 8) + row // 8] = 1
    row = np.arange(512)
    pick_two = np.zeros((512, 64), np.float32)
    pick_two[row, 8 * (row % 8) + ((row >> 4) & 7)] = 1
    row = np.arange(128)
    pick_three = np.zeros((128, 64), np.float32)
    pick_three[row, 8 * (4 * bit(row, 5) + 2 * bit(row, 3) + bit(row, 0))] = 1
    return [np.asarray(each, jnp.bfloat16) for each in (pick_one, pick_two, pick_three)]


def slot_tables():
    slot = np.arange(128)
    y_part = 2 * (slot // 32) + slot % 2
    z_part = (slot // 2) % 16
    mode = np.arange(128)
    kz, ky = mode // 8, mode % 8
    angle = np.outer(kz, z_part) / 16 + np.outer(ky, y_part) / 8
    angle = 2 * np.pi * (angle[None] + kz[None, :, None] * np.arange(16)[:, None, None] / 256)
    high, low = two_terms(np.concatenate([np.cos(angle), np.sin(angle)], axis=2))
    both = np.concatenate([high, low], axis=1)
    turn = 2 * np.pi * np.outer(np.arange(4), y_part) / 32
    turns = np.stack([np.cos(turn), np.sin(turn)]).astype(np.float32)
    return both, turns


def line_tables():
    z_low, kz_high = np.arange(128), np.arange(128)
    sign = 1 - 2 * (kz_high % 2)
    ahead, back = [], []
    for kz_low in range(16):
        angle = 2 * np.pi * np.outer(z_low, kz_low + 16 * kz_high) / 2048
        cos, sin = np.cos(angle), np.sin(angle)
        back.append(np.block([[cos, -sin], [sin, cos]]))
        angle = np.outer(z_low, kz_high) / 128 + (z_low % 8)[:, None] * kz_low / 2048
        cos, sin = np.cos(2 * np.pi * angle), np.sin(2 * np.pi * angle)
        ahead.append(np.block([[cos, -sin], [sin * sign, cos * sign]]))
    pair = lambda a: np.stack(two_terms(np.stack(a)), axis=1)
    return pair(ahead), pair(back)


def turn_tables():
    kt = np.arange(4)[:, None]
    s = np.arange(8)[None, :]
    ky_low = kt + 4 * s
    one = 2 * np.pi * ky_low[:, None, :] * np.arange(8)[None, :, None] / 256
    mode = ky_low[:, None, None, :] + 32 * np.arange(8)[None, None, :, None]
    two = 2 * np.pi * mode * np.arange(8)[None, :, None, None] / 2048
    wide = lambda a: np.ascontiguousarray(
        np.broadcast_to(np.stack([np.cos(a), np.sin(a)])[..., None], (2,) + a.shape + (128,))
    ).astype(np.float32)
    moved = two[..., None] - 2 * np.pi * np.multiply.outer(np.arange(8), np.arange(128))[
        None, :, None, None, :] / 16
    moved = np.stack([np.cos(moved), np.sin(moved)]).astype(np.float32)
    return wide(one), wide(two), moved


def digit_tables():
    out = []
    for pair in range(2):
        full = np.zeros((2, 2, 8, 8, 2, 2, 8, 8))
        for k in range(2):
            y2a = np.arange(8)[:, None]
            s = np.arange(8)[None, :]
            angle = 2 * np.pi * (s * y2a / 8 + (2 * pair + k) * y2a / 32)
            cos, sin = np.cos(angle), np.sin(angle)
            for y0 in range(8):
                full[0, k, :, y0, 0, k, y0, :] = cos
                full[0, k, :, y0, 1, k, y0, :] = -sin
                full[1, k, :, y0, 0, k, y0, :] = sin
                full[1, k, :, y0, 1, k, y0, :] = cos
        high, low = two_terms(full.reshape(256, 256))
        out.append(np.concatenate([high, low], axis=0))
    return np.stack(out)


def split(x):
    high = x.astype(BF16)
    return high, (x - high.astype(F32)).astype(BF16)


def dot(a, b):
    return jnp.dot(a, b, preferred_element_type=F32)


def dot_nt(a, b):
    return lax.dot_general(a, b, (((1,), (1,)), ((), ())), preferred_element_type=F32)


def add(a, b):
    return (a[0] + b[0], a[1] + b[1])


def sub(a, b):
    return (a[0] - b[0], a[1] - b[1])


def times(a, cos, sin, sign):
    if sign > 0:
        return (a[0] * cos - a[1] * sin, a[1] * cos + a[0] * sin)
    return (a[0] * cos + a[1] * sin, a[1] * cos - a[0] * sin)


def quarter(a, sign):
    return (-a[1], a[0]) if sign > 0 else (a[1], -a[0])


def add_quarter(a, b, sign):
    return (a[0] - b[1], a[1] + b[0]) if sign > 0 else (a[0] + b[1], a[1] - b[0])


def four(x, sign):
    even, odd = add(x[0], x[2]), add(x[1], x[3])
    left, right = sub(x[0], x[2]), sub(x[1], x[3])
    return [add(even, odd), add_quarter(left, right, sign), sub(even, odd),
            add_quarter(left, right, -sign)]


def eight(x, sign):
    even = four([x[0], x[2], x[4], x[6]], sign)
    odd = four([x[1], x[3], x[5], x[7]], sign)
    half = math.sqrt(0.5)
    a = odd[1]
    if sign > 0:
        odd1 = ((a[0] - a[1]) * half, (a[1] + a[0]) * half)
    else:
        odd1 = ((a[0] + a[1]) * half, (a[1] - a[0]) * half)
    a = odd[3]
    if sign > 0:
        odd3 = ((-a[0] - a[1]) * half, (a[0] - a[1]) * half)
    else:
        odd3 = ((a[1] - a[0]) * half, (-a[0] - a[1]) * half)
    return [
        add(even[0], odd[0]),
        add(even[1], odd1),
        add_quarter(even[2], odd[2], sign),
        add(even[3], odd3),
        sub(even[0], odd[0]),
        sub(even[1], odd1),
        add_quarter(even[2], odd[2], -sign),
        sub(even[3], odd3),
    ]


def sixteen(x, sign):
    out = [None] * 16
    mid = [four([x[a], x[a + 4], x[a + 8], x[a + 12]], sign) for a in range(4)]
    for c in range(4):
        terms = []
        for a in range(4):
            angle = 2 * math.pi * a * c / 16
            if a * c == 0:
                terms.append(mid[a][c])
            elif a * c == 4:
                terms.append(quarter(mid[a][c], sign))
            else:
                terms.append(times(mid[a][c], math.cos(angle), math.sin(angle), sign))
        done = four(terms, sign)
        for d in range(4):
            out[c + 4 * d] = done[d]
    return out


def spread(rows, width, own):
    shape = (64, 64 * width)
    column = lax.broadcasted_iota(jnp.int32, shape, 1) // width
    source = lax.broadcasted_iota(jnp.int32, shape, 0)
    wide = dot(rows.astype(BF16), (((column + 8) & 63) == source).astype(F32).astype(BF16))
    shape = (rows.shape[0], 64 * width)
    cell = lax.broadcasted_iota(jnp.int32, shape, 1) & (width - 1)
    return jnp.where(cell == own(lax.broadcasted_iota(jnp.int32, shape, 0)), wide, 0.0).astype(BF16)


def prepare(mixing, picks, first_map, second_map, leaf_map):
    mix = mixing[...]
    first_map[...] = dot(picks[0][...], mix).astype(BF16)
    second_map[...] = spread(dot(picks[1][...], mix), 8, lambda r: 2 * (r >> 7) + bit(r, 3))
    leaf_map[...] = spread(
        dot(picks[2][...], mix), 16,
        lambda r: 8 * bit(r, 2) + 4 * bit(r, 6) + 2 * bit(r, 4) + bit(r, 1))


def expand(half, digit, lanes, top, one, two, draws, arrived_draws, first_map, second_map, leaf_map,
           slots, turns, parents, leaves, high_rows, low_rows, sent):
    records = jnp.concatenate([top[:, lanes], one[:, lanes].astype(F32)], axis=0)
    high, low = split(records)
    high, low = split(dot(first_map[...], high) + dot(first_map[...], low))
    level_two = dot(second_map[...], jnp.concatenate([two[half], high], axis=0))
    low = jnp.concatenate([jnp.zeros_like(low), low], axis=0)
    level_two = level_two + dot(second_map[:, 384:], low)
    for tile in range(4):
        high, low = split(level_two[tile * 128:(tile + 1) * 128])
        parents[tile, 0:128] = high
        parents[tile, 128:256] = low

    @pl.loop(0, 2)
    def _(c1x):
        for c1y in range(2):
            tile = 2 * c1x + c1y
            arrived_draws(half, tile).wait()
            rows = pl.ds(pl.multiple_of(tile * 16, 16), 16)
            got = dot(leaf_map[:, :896], draws[half, :, rows, :].reshape(896, 512))
            near = parents[tile]
            got = got + dot(leaf_map[:, 896:], near[:128]) + dot(leaf_map[:, 896:], near[128:])
            for group in range(4):
                for i in range(4):
                    row = group * 32 + i * 8
                    leaves[group // 2, group % 2, 4 * c1y + i] = got[row:row + 8]

        @pl.loop(0, 8)
        def _(twin):
            for pair in range(2):
                quarters = []
                for t in range(4):
                    lane = slice(t * 128, t * 128 + 128)
                    first, second = [], []
                    for j in range(2):
                        group = lax.rem(2 * twin + j - digit + 16, 16)
                        part, oy = group // 8, lax.rem(group, 8)
                        first.append(leaves[pair, part, oy, :, lane])
                        other = leaves[pair, 1 - part, oy, :, lane]
                        second.append(other * (1 - 2 * part).astype(F32))
                    quarters.append((jnp.concatenate(first, axis=0), jnp.concatenate(second, axis=0)))
                rows = pl.ds(pl.multiple_of(pair * 128 + twin * 16, 16), 16)
                for k, value in enumerate(four(quarters, -1)):
                    if k:
                        value = times(value, turns[0, k:k + 1], turns[1, k:k + 1], -1)
                    for side in range(2):
                        high, low = split(value[side])
                        high_rows[k, rows, side * 128:side * 128 + 128] = high
                        low_rows[k, rows, side * 128:side * 128 + 128] = low

        for k in range(4):
            both = dot_nt(slots[...], high_rows[k])
            done = both[:128] + both[128:] + dot_nt(slots[0:128], low_rows[k])
            for pair in range(2):
                piece = done[:, pair * 128:(pair + 1) * 128].reshape(16, 8, 128)
                sent[half, 2 * c1x + pair, :, k] = piece


def owner_index(q, w):
    index = 0
    for b in range(4):
        index += bit(w, b) << (2 * b)
    for b in range(3):
        index += bit(q, b) << (2 * b + 1)
    return index


def gather_lanes(x, lane):
    for b in range(4):
        here = (lane & (8 << b)) != 0
        x = [jnp.where(here, x[(m + (1 << b)) % 16], x[m]) for m in range(16)]
    return [x[(16 - d) % 16] for d in range(16)]


def along_lines(kt, arrived, factor, table, turn_one, turn_two, moved, lane, flat, mid, work, placed):
    @pl.loop(0, 8, unroll=2)
    def _(q):
        base = 2 * (q % 2) + 8 * ((q // 2) % 2) + 32 * (q // 4)
        places = [owner_index(0, w) for w in range(16)]
        got = gather_lanes([arrived[base + place, kt] for place in places], lane)
        for oy in range(8):
            rows = pl.ds(pl.multiple_of(q * 64 + oy * 8, 8), 8)
            flat[rows, 0:128] = got[oy]
            flat[rows, 128:256] = got[8 + oy]

    for part in range(2):
        rows = pl.ds(part * 256, 256)
        high, low = split(flat[rows, :])
        mid[rows, :] = dot(high, table[0]) + dot(low, table[0]) + dot(high, table[1])

    @pl.loop(0, 8, unroll=2)
    def _(oy):
        x = []
        for q in range(8):
            rows = pl.ds(pl.multiple_of(q * 64 + oy * 8, 8), 8)
            value = (mid[rows, 0:128], mid[rows, 128:256])
            if q:
                value = times(value, turn_one[0, kt, q], turn_one[1, kt, q], -1)
            x.append(value)
        for k, value in enumerate(eight(x, -1)):
            value = times(value, moved[0, kt, oy, k], moved[1, kt, oy, k], -1)
            work[0, k, oy] = value[0]
            work[1, k, oy] = value[1]

    @pl.loop(0, 8, unroll=2)
    def _(kq):
        x = eight([(work[0, kq, oy], work[1, kq, oy]) for oy in range(8)], -1)
        y = []
        for k in range(8):
            rows = pl.ds(pl.multiple_of((kt * 8 + k) * 64 + kq * 8, 8), 8)
            scale = factor[rows, :]
            y.append((x[k][0] * scale, x[k][1] * scale))
        for y0, value in enumerate(eight(y, 1)):
            value = times(value, turn_two[0, kt, y0, kq], turn_two[1, kt, y0, kq], 1)
            work[0, kq, y0] = value[0]
            work[1, kq, y0] = value[1]

    @pl.loop(0, 8, unroll=2)
    def _(y0):
        x = [(work[0, kq, y0], work[1, kq, y0]) for kq in range(8)]
        for y1, value in enumerate(eight(x, 1)):
            if y1:
                value = times(value, turn_one[0, kt, y1], turn_one[1, kt, y1], 1)
            placed[0, kt, y1, y0] = value[0]
            placed[1, kt, y1, y0] = value[1]


def next_digit(ktp, digits, placed, mixed):
    @pl.loop(0, 4, unroll=True)
    def _(pair):
        columns = []
        for one in range(2):
            pieces = [
                placed[part, 2 * ktp + k, 2 * pair + one].reshape(64, 128)
                for part in range(2)
                for k in range(2)
            ]
            columns.append(jnp.concatenate(pieces, axis=0))
        high, low = split(jnp.concatenate(columns, axis=1))
        both = dot(digits[ktp], high)
        mixed[ktp, pair] = both[:256] + both[256:] + dot(digits[ktp, 0:256], low)


def last_digit(odd, mixed, lined):
    @pl.loop(0, 4, unroll=True)
    def _(pair):
        for y2a in range(odd, 8, 2):
            for one in range(2):
                x = []
                for kt in range(4):
                    base = (kt % 2) * 64 + y2a * 8
                    lanes = slice(one * 128, one * 128 + 128)
                    x.append((mixed[kt // 2, pair, base:base + 8, lanes],
                              mixed[kt // 2, pair, 128 + base:128 + base + 8, lanes]))
                for y2b, value in enumerate(four(x, 1)):
                    rows = pl.ds(pl.multiple_of((y2b * 8 + y2a) * 64 + (2 * pair + one) * 8, 8), 8)
                    lined[rows, 0:128] = value[0]
                    lined[rows, 128:256] = value[1]


PHASES = ((0, 3), (3, 1))


def whole_kernel(top, one, mixing, *refs):
    picks, refs = refs[:3], refs[3:]
    (turns, three, two_far, digits_far, slots_far, transfer, ahead_far, back_far, turn_one_far, turn_two_far,
     moved_far, out,
     first_map, second_map, leaf_map, two, digits, draws, parents, leaves, high_rows, low_rows, sent, arrived,
     slots, modes, factor, ahead, back, turn_one, turn_two, moved, flat, mid, work, placed, mixed, lined, ready,
          draw_sem, fetch_sem, send_sem, recv_sem, back_send, back_recv,
     two_sem) = refs
    row, col = lax.axis_index("row"), lax.axis_index("col")
    me = row * 16 + col
    core, z, y_low = lax.rem(col, 2), lax.rem(col // 2, 4), col // 8
    x, y_high = lax.rem(row, 4), row // 4

    digit = (lax.rem(col, 2) + 2 * lax.rem(col // 4, 2) + 4 * lax.rem(row, 2)
             + 8 * lax.rem(row // 4, 2))

    barrier = pltpu.get_barrier_semaphore()

    @pl.loop(1, 128)
    def _(k):
        other = lax.rem(me + k, 128)
        pl.semaphore_signal(barrier, inc=1, device_id=(other // 16, lax.rem(other, 16)),
                            device_id_type=MESH)

    def lanes_of(half):
        e = lax.rem(half + core, 2)
        return pl.ds(pl.multiple_of(e * 512, 512), 512)

    def draw_copy(half, tile):
        rows = pl.ds(pl.multiple_of(tile * 16, 16), 16)
        return pltpu.make_async_copy(three.at[:, rows, lanes_of(half)],
                                     draws.at[half, :, rows, :], draw_sem.at[half, tile])

    fetch_slots = pltpu.make_async_copy(slots_far.at[digit], slots, fetch_sem.at[6])
    fetch_slots.start()
    def two_copy(half):
        return pltpu.make_async_copy(two_far.at[:, lanes_of(half)], two.at[half], two_sem.at[half])

    for half in range(2):
        two_copy(half).start()
        for tile in range(4):
            draw_copy(half, tile).start()
    fetches = [
        pltpu.make_async_copy(transfer, modes, fetch_sem.at[0]),
        pltpu.make_async_copy(ahead_far.at[col], ahead, fetch_sem.at[1]),
        pltpu.make_async_copy(back_far.at[col], back, fetch_sem.at[4]),
        pltpu.make_async_copy(moved_far, moved, fetch_sem.at[5]),
        pltpu.make_async_copy(digits_far, digits, fetch_sem.at[7]),
        pltpu.make_async_copy(turn_one_far, turn_one, fetch_sem.at[2]),
        pltpu.make_async_copy(turn_two_far, turn_two, fetch_sem.at[3]),
    ]
    prepare(mixing, picks, first_map, second_map, leaf_map)
    fetch_slots.wait()

    def send(half, phase):
        first, count = PHASES[phase]
        kts = pl.ds(first, count)
        e = lax.rem(half + core, 2)

        @pl.loop(0, 64)
        def _(k):
            j = lax.rem(k * 37 + 37, 64)
            to_x = lax.rem(x + lax.rem(j, 4), 4)
            to_z = lax.rem(z + lax.rem(j // 4, 4), 4)
            to_y = lax.rem(y_low + lax.rem(j // 16, 2), 2)
            to_core = lax.rem(core + j // 32, 2)
            to_row, to_col = 4 * e + to_x, to_y * 8 + to_z * 2 + to_core
            here = jnp.logical_and(to_row == row, to_col == col)

            @pl.when(jnp.logical_not(here))
            def _():
                pltpu.make_async_remote_copy(
                    sent.at[half, to_x, to_col, kts], arrived.at[me, kts],
                    send_sem.at[half, phase], recv_sem.at[phase],
                    device_id=(to_row, to_col), device_id_type=MESH).start()

            @pl.when(here)
            def _():
                pltpu.make_async_copy(sent.at[half, to_x, to_col, kts], arrived.at[me, kts],
                                      send_sem.at[half, phase]).start()

    def sent_all(half, phase):
        first, count = PHASES[phase]
        view = sent.at[half, :, :, pl.ds(first, count)]
        pltpu.make_async_copy(view, view, send_sem.at[half, phase]).wait()

    def received_all(phase):
        first, count = PHASES[phase]
        view = arrived.at[pl.ds(0, 127), pl.ds(first, count)]
        pltpu.make_async_copy(view, view, recv_sem.at[phase]).wait()

    for half in range(2):
        two_copy(half).wait()
        expand(half, digit, lanes_of(half), top, one, two, draws, draw_copy, first_map, second_map,
               leaf_map, slots, turns, parents, leaves, high_rows, low_rows, sent)
        if half == 0:
            pl.semaphore_wait(barrier, 127)
        send(half, 0)
        if half == 0:
            for fetch in fetches:
                fetch.start()

    for fetch in fetches:
        fetch.wait()

    @pl.loop(0, 128)
    def _(i):
        low, kt, high = i // 32, lax.rem(i // 8, 4), lax.rem(i, 8)
        rows = modes[pl.ds(pl.multiple_of((low * 4 + kt) * 128 + high * 16, 16), 16), :]
        factor[pl.ds((kt * 8 + high) * 64 + low, 16, stride=4), :] = rows * (1.0 / (2048 * 2048))

    sent_all(0, 0)
    send(0, 1)
    sent_all(1, 0)
    send(1, 1)

    lane = lax.broadcasted_iota(jnp.int32, (8, 128), 1)
    for phase in range(2):
        if phase:
            sent_all(0, 1)
            sent_all(1, 1)
        received_all(phase)
        first, count = PHASES[phase]

        @pl.loop(first, first + count)
        def _(kt):
            along_lines(kt, arrived, factor, ahead, turn_one, turn_two, moved, lane, flat, mid, work,
                        placed)

        next_digit(phase, digits, placed, mixed)

    for odd in range(2):
        last_digit(odd, mixed, lined)
        half_strip = pl.ds(odd * 64, 64)

        @pl.loop(0, 16)
        def _(k):
            j = lax.rem(k * 7 + 7, 16)
            to_z = lax.rem(z + lax.rem(j // 2, 4), 4)
            to_y = lax.rem(y_low + lax.rem(j, 2), 2)
            to_core = lax.rem(core + j // 8, 2)
            to = to_y * 8 + to_z * 2 + to_core
            rows = pl.ds(pl.multiple_of(to * 128 + odd * 64, 64), 64)
            high, low = split(lined[rows, :])
            both = dot_nt(jnp.concatenate([high, low], axis=0), back[0])
            done = both[:64] + both[64:] + dot_nt(high, back[1])
            ready[to, 0, half_strip, :] = done[:, :128]
            ready[to, 1, half_strip, :] = done[:, 128:]
            source = ready.at[to, :, half_strip, :]
            target = out.at[col, :, half_strip, :]

            @pl.when(to != col)
            def _():
                pltpu.make_async_remote_copy(
                    source, target, back_send.at[odd], back_recv.at[odd],
                    device_id=(row, to), device_id_type=MESH).start()

            @pl.when(to == col)
            def _():
                pltpu.make_async_copy(source, target, back_send.at[odd]).start()

    for odd in range(2):
        half_strip = pl.ds(odd * 64, 64)
        view = ready.at[:, :, half_strip, :]
        pltpu.make_async_copy(view, view, back_send.at[odd]).wait()
        view = ready.at[pl.ds(0, 15), :, half_strip, :]
        pltpu.make_async_copy(view, view, back_recv.at[odd]).wait()


def strip_kernel(arrived, out, near, strip, sem, out_sem):
    def fetch(part):
        rows = pl.ds(part * 32, 32)
        return [
            pltpu.make_async_copy(arrived.at[pl.ds(8 * k, 8), :, rows, :],
                                  near.at[pl.ds(8 * k, 8), :, rows, :], sem.at[part, k])
            for k in range(2)
        ]

    def put(part):
        rows = pl.ds(part * 32, 32)
        return [
            pltpu.make_async_copy(strip.at[plane, rows, :], out.at[plane, rows, :],
                                  out_sem.at[part, plane])
            for plane in range(2)
        ]

    for part in range(4):
        for copy in fetch(part):
            copy.start()
    for part in range(4):
        for copy in fetch(part):
            copy.wait()

        @pl.loop(0, 4, unroll=2)
        def _(tile):
            rows = pl.ds(pl.multiple_of(part * 32 + tile * 8, 8), 8)
            x = [(near[k, 0, rows, :], near[k, 1, rows, :]) for k in range(16)]
            for place, value in enumerate(sixteen(x, 1)):
                strip[0, rows, place * 128:(place + 1) * 128] = value[0]
                strip[1, rows, place * 128:(place + 1) * 128] = value[1]

        for copy in put(part):
            copy.start()
    for part in range(4):
        for copy in put(part):
            copy.wait()


def body(*arrays):
    outside = pl.BlockSpec(memory_space=pl.ANY)
    return pl.pallas_call(
        strip_kernel,
        in_specs=[outside],
        out_specs=outside,
        out_shape=jax.ShapeDtypeStruct((2, 128, 2048), F32),
        scratch_shapes=[
            VMEM((16, 2, 128, 128), F32),
            VMEM((2, 128, 2048), F32),
            pltpu.SemaphoreType.DMA((4, 2)),
            pltpu.SemaphoreType.DMA((4, 2)),
        ],
        compiler_params=pltpu.CompilerParams(vmem_limit_bytes=60 * 2**20),
    )(whole(*arrays))


def whole(top, one, two, three, mixing, transfer):
    slots, turns = slot_tables()
    turn_one, turn_two, moved = turn_tables()
    ahead, back = line_tables()
    near = [top, one, mixing] + owner_tables()
    near += [turns]
    far = [three, two.reshape(448, 1024), digit_tables(), slots, transfer, ahead, back, turn_one, turn_two, moved]
    inside, outside = pl.BlockSpec(memory_space=VMEM), pl.BlockSpec(memory_space=pl.ANY)
    dma = pltpu.SemaphoreType.DMA
    return pl.pallas_call(
        whole_kernel,
        in_specs=[inside] * len(near) + [outside] * len(far),
        out_specs=outside,
        out_shape=jax.ShapeDtypeStruct((16, 2, 128, 128), F32),
        scratch_shapes=[
            VMEM((64, 64), BF16),
            VMEM((512, 512), BF16),
            VMEM((128, 1024), BF16),
            VMEM((2, 448, 512), BF16),
            VMEM((2, 512, 256), BF16),
            VMEM((2, 56, 64, 512), BF16),
            VMEM((4, 256, 512), BF16),
            VMEM((2, 2, 8, 8, 512), F32),
            VMEM((4, 256, 256), BF16),
            VMEM((4, 256, 256), BF16),
            VMEM((2, 4, 16, 4, 8, 128), F32),
            VMEM((128, 4, 8, 128), F32),
            VMEM((256, 256), BF16),
            VMEM((2048, 128), F32),
            VMEM((2056, 128), F32),
            VMEM((2, 256, 256), BF16),
            VMEM((2, 256, 256), BF16),
            VMEM((2, 4, 8, 8, 128), F32),
            VMEM((2, 4, 8, 8, 8, 128), F32),
            VMEM((2, 4, 8, 8, 8, 128), F32),
            VMEM((512, 256), F32),
            VMEM((512, 256), F32),
            VMEM((2, 8, 8, 8, 128), F32),
            VMEM((2, 4, 8, 8, 8, 128), F32),
            VMEM((2, 4, 256, 256), F32),
            VMEM((2048, 256), F32),
            VMEM((16, 2, 128, 128), F32),
            dma((2, 4)),
            dma((8,)),
            dma((2, 2)),
            dma((2,)),
            dma((2,)),
            dma((2,)),
            dma((2,)),
        ],
        compiler_params=pltpu.CompilerParams(
            collective_id=0, has_side_effects=True, vmem_limit_bytes=56 * 2**20),
    )(*[jnp.asarray(a) for a in near + far])


def solution(mesh):
    return jax.shard_map(
        body,
        mesh=mesh,
        in_specs=(
            P(None, ("row", "col")),
            P(None, ("row", "col")),
            P(None, None, ("row", "col")),
            P(None, None, ("row", "col")),
            P(),
            P(None, "col"),
        ),
        out_specs=P("row", "col", None),
        check_vma=False,
    )
```

```python
import math

import jax
import jax.numpy as jnp
import numpy as np
from jax import lax
from jax.experimental import pallas as pl
from jax.experimental.pallas import tpu as pltpu
from jax.sharding import PartitionSpec as P

F32 = jnp.float32
BF16 = jnp.bfloat16
VMEM = pltpu.VMEM
MESH = pl.DeviceIdType.MESH


def two_terms(values):
    values = np.asarray(values, np.float32)
    high = values.astype(jnp.bfloat16)
    low = (values - high.astype(np.float32)).astype(jnp.bfloat16)
    return high, low


def bit(value, index):
    return (value >> index) & 1


def owner_tables():
    row = np.arange(64)
    pick_one = np.zeros((64, 64), np.float32)
    pick_one[row, 8 * (row % 8) + row // 8] = 1
    row = np.arange(512)
    pick_two = np.zeros((512, 64), np.float32)
    pick_two[row, 8 * (row % 8) + ((row >> 4) & 7)] = 1
    row = np.arange(128)
    pick_three = np.zeros((128, 64), np.float32)
    pick_three[row, 8 * (4 * bit(row, 5) + 2 * bit(row, 3) + bit(row, 0))] = 1
    return [np.asarray(each, jnp.bfloat16) for each in (pick_one, pick_two, pick_three)]


def slot_tables():
    slot = np.arange(128)
    y_part = 2 * (slot // 32) + slot % 2
    z_part = (slot // 2) % 16
    mode = np.arange(128)
    kz, ky = mode // 8, mode % 8
    angle = np.outer(kz, z_part) / 16 + np.outer(ky, y_part) / 8
    angle = 2 * np.pi * (angle[None] + kz[None, :, None] * np.arange(16)[:, None, None] / 256)
    high, low = two_terms(np.concatenate([np.cos(angle), np.sin(angle)], axis=2))
    both = np.concatenate([high, low], axis=1)
    turn = 2 * np.pi * np.outer(np.arange(4), y_part) / 32
    turns = np.stack([np.cos(turn), np.sin(turn)]).astype(np.float32)
    return both, turns


def line_tables():
    z_low, kz_high = np.arange(128), np.arange(128)
    sign = 1 - 2 * (kz_high % 2)
    ahead, back = [], []
    for kz_low in range(16):
        angle = 2 * np.pi * np.outer(z_low, kz_low + 16 * kz_high) / 2048
        cos, sin = np.cos(angle), np.sin(angle)
        back.append(np.block([[cos, -sin], [sin, cos]]))
        angle = np.outer(z_low, kz_high) / 128 + (z_low % 8)[:, None] * kz_low / 2048
        cos, sin = np.cos(2 * np.pi * angle), np.sin(2 * np.pi * angle)
        ahead.append(np.block([[cos, -sin], [sin * sign, cos * sign]]))
    pair = lambda a: np.stack(two_terms(np.stack(a)), axis=1)
    return pair(ahead), pair(back)


def turn_tables():
    kt = np.arange(4)[:, None]
    s = np.arange(8)[None, :]
    ky_low = kt + 4 * s
    one = 2 * np.pi * ky_low[:, None, :] * np.arange(8)[None, :, None] / 256
    mode = ky_low[:, None, None, :] + 32 * np.arange(8)[None, None, :, None]
    two = 2 * np.pi * mode * np.arange(8)[None, :, None, None] / 2048
    wide = lambda a: np.ascontiguousarray(
        np.broadcast_to(np.stack([np.cos(a), np.sin(a)])[..., None], (2,) + a.shape + (128,))
    ).astype(np.float32)
    moved = two[..., None] - 2 * np.pi * np.multiply.outer(np.arange(8), np.arange(128))[
        None, :, None, None, :] / 16
    moved = np.stack([np.cos(moved), np.sin(moved)]).astype(np.float32)
    return wide(one), wide(two), moved


def digit_tables():
    out = []
    for pair in range(2):
        full = np.zeros((2, 2, 8, 8, 2, 2, 8, 8))
        for k in range(2):
            y2a = np.arange(8)[:, None]
            s = np.arange(8)[None, :]
            angle = 2 * np.pi * (s * y2a / 8 + (2 * pair + k) * y2a / 32)
            cos, sin = np.cos(angle), np.sin(angle)
            for y0 in range(8):
                full[0, k, :, y0, 0, k, y0, :] = cos
                full[0, k, :, y0, 1, k, y0, :] = -sin
                full[1, k, :, y0, 0, k, y0, :] = sin
                full[1, k, :, y0, 1, k, y0, :] = cos
        high, low = two_terms(full.reshape(256, 256))
        out.append(np.concatenate([high, low], axis=0))
    return np.stack(out)


def split(x):
    high = x.astype(BF16)
    return high, (x - high.astype(F32)).astype(BF16)


def dot(a, b):
    return jnp.dot(a, b, preferred_element_type=F32)


def dot_nt(a, b):
    return lax.dot_general(a, b, (((1,), (1,)), ((), ())), preferred_element_type=F32)


def add(a, b):
    return (a[0] + b[0], a[1] + b[1])


def sub(a, b):
    return (a[0] - b[0], a[1] - b[1])


def times(a, cos, sin, sign):
    if sign > 0:
        return (a[0] * cos - a[1] * sin, a[1] * cos + a[0] * sin)
    return (a[0] * cos + a[1] * sin, a[1] * cos - a[0] * sin)


def quarter(a, sign):
    return (-a[1], a[0]) if sign > 0 else (a[1], -a[0])


def add_quarter(a, b, sign):
    return (a[0] - b[1], a[1] + b[0]) if sign > 0 else (a[0] + b[1], a[1] - b[0])


def four(x, sign):
    even, odd = add(x[0], x[2]), add(x[1], x[3])
    left, right = sub(x[0], x[2]), sub(x[1], x[3])
    return [add(even, odd), add_quarter(left, right, sign), sub(even, odd),
            add_quarter(left, right, -sign)]


def eight(x, sign):
    even = four([x[0], x[2], x[4], x[6]], sign)
    odd = four([x[1], x[3], x[5], x[7]], sign)
    half = math.sqrt(0.5)
    a = odd[1]
    if sign > 0:
        odd1 = ((a[0] - a[1]) * half, (a[1] + a[0]) * half)
    else:
        odd1 = ((a[0] + a[1]) * half, (a[1] - a[0]) * half)
    a = odd[3]
    if sign > 0:
        odd3 = ((-a[0] - a[1]) * half, (a[0] - a[1]) * half)
    else:
        odd3 = ((a[1] - a[0]) * half, (-a[0] - a[1]) * half)
    return [
        add(even[0], odd[0]),
        add(even[1], odd1),
        add_quarter(even[2], odd[2], sign),
        add(even[3], odd3),
        sub(even[0], odd[0]),
        sub(even[1], odd1),
        add_quarter(even[2], odd[2], -sign),
        sub(even[3], odd3),
    ]


def sixteen(x, sign):
    out = [None] * 16
    mid = [four([x[a], x[a + 4], x[a + 8], x[a + 12]], sign) for a in range(4)]
    for c in range(4):
        terms = []
        for a in range(4):
            angle = 2 * math.pi * a * c / 16
            if a * c == 0:
                terms.append(mid[a][c])
            elif a * c == 4:
                terms.append(quarter(mid[a][c], sign))
            else:
                terms.append(times(mid[a][c], math.cos(angle), math.sin(angle), sign))
        done = four(terms, sign)
        for d in range(4):
            out[c + 4 * d] = done[d]
    return out


def spread(rows, width, own):
    shape = (64, 64 * width)
    column = lax.broadcasted_iota(jnp.int32, shape, 1) // width
    source = lax.broadcasted_iota(jnp.int32, shape, 0)
    wide = dot(rows.astype(BF16), (((column + 8) & 63) == source).astype(F32).astype(BF16))
    shape = (rows.shape[0], 64 * width)
    cell = lax.broadcasted_iota(jnp.int32, shape, 1) & (width - 1)
    return jnp.where(cell == own(lax.broadcasted_iota(jnp.int32, shape, 0)), wide, 0.0).astype(BF16)


def prepare(mixing, picks, first_map, second_map, leaf_map):
    mix = mixing[...]
    first_map[...] = dot(picks[0][...], mix).astype(BF16)
    second_map[...] = spread(dot(picks[1][...], mix), 8, lambda r: 2 * (r >> 7) + bit(r, 3))
    leaf_map[...] = spread(
        dot(picks[2][...], mix), 16,
        lambda r: 8 * bit(r, 2) + 4 * bit(r, 6) + 2 * bit(r, 4) + bit(r, 1))


def expand(half, digit, lanes, top, one, two, draws, arrived_draws, first_map, second_map, leaf_map,
           slots, turns, parents, leaves, high_rows, low_rows, sent, fetch_half):
    records = jnp.concatenate([top[:, lanes], one[:, lanes].astype(F32)], axis=0)
    high, low = split(records)
    high, low = split(dot(first_map[...], high) + dot(first_map[...], low))
    level_two = dot(second_map[...], jnp.concatenate([two[half], high], axis=0))
    low = jnp.concatenate([jnp.zeros_like(low), low], axis=0)
    level_two = level_two + dot(second_map[:, 384:], low)
    for tile in range(4):
        high, low = split(level_two[tile * 128:(tile + 1) * 128])
        parents[tile, 0:128] = high
        parents[tile, 128:256] = low

    if half == 0:
        fetch_half(1)

    @pl.loop(0, 2)
    def _(c1x):
        for c1y in range(2):
            tile = 2 * c1x + c1y
            arrived_draws(half, tile).wait()
            rows = pl.ds(pl.multiple_of(tile * 16, 16), 16)
            got = dot(leaf_map[:, :896], draws[half, :, rows, :].reshape(896, 512))
            near = parents[tile]
            got = got + dot(leaf_map[:, 896:], near[:128]) + dot(leaf_map[:, 896:], near[128:])
            for group in range(4):
                for i in range(4):
                    row = group * 32 + i * 8
                    leaves[group // 2, group % 2, 4 * c1y + i] = got[row:row + 8]

        @pl.loop(0, 8, unroll=4)
        def _(twin):
            for pair in range(2):
                quarters = []
                for t in range(4):
                    lane = slice(t * 128, t * 128 + 128)
                    first, second = [], []
                    for j in range(2):
                        group = lax.rem(2 * twin + j - digit + 16, 16)
                        part, oy = group // 8, lax.rem(group, 8)
                        first.append(leaves[pair, part, oy, :, lane])
                        other = leaves[pair, 1 - part, oy, :, lane]
                        second.append(other * (1 - 2 * part).astype(F32))
                    quarters.append((jnp.concatenate(first, axis=0), jnp.concatenate(second, axis=0)))
                rows = pl.ds(pl.multiple_of(pair * 128 + twin * 16, 16), 16)
                for k, value in enumerate(four(quarters, -1)):
                    if k:
                        value = times(value, turns[0, k:k + 1], turns[1, k:k + 1], -1)
                    for side in range(2):
                        high, low = split(value[side])
                        high_rows[k, rows, side * 128:side * 128 + 128] = high
                        low_rows[k, rows, side * 128:side * 128 + 128] = low

        for k in range(4):
            both = dot_nt(slots[...], high_rows[k])
            done = both[:128] + both[128:] + dot_nt(slots[0:128], low_rows[k])
            for pair in range(2):
                piece = done[:, pair * 128:(pair + 1) * 128].reshape(16, 8, 128)
                sent[half, 2 * c1x + pair, :, k] = piece


def owner_index(q, w):
    index = 0
    for b in range(4):
        index += bit(w, b) << (2 * b)
    for b in range(3):
        index += bit(q, b) << (2 * b + 1)
    return index


def gather_lanes(x, lane):
    for b in range(4):
        here = (lane & (8 << b)) != 0
        x = [jnp.where(here, x[(m + (1 << b)) % 16], x[m]) for m in range(16)]
    return [x[(16 - d) % 16] for d in range(16)]


def along_lines(kt, arrived, factor, table, turn_one, turn_two, moved, lane, flat, mid, work, placed):
    @pl.loop(0, 8, unroll=2)
    def _(q):
        base = 2 * (q % 2) + 8 * ((q // 2) % 2) + 32 * (q // 4)
        places = [owner_index(0, w) for w in range(16)]
        got = gather_lanes([arrived[base + place, kt] for place in places], lane)
        for oy in range(8):
            rows = pl.ds(pl.multiple_of(q * 64 + oy * 8, 8), 8)
            flat[rows, 0:128] = got[oy]
            flat[rows, 128:256] = got[8 + oy]

    for part in range(2):
        rows = pl.ds(part * 256, 256)
        high, low = split(flat[rows, :])
        mid[rows, :] = dot(high, table[0]) + dot(low, table[0]) + dot(high, table[1])

    @pl.loop(0, 8, unroll=2)
    def _(oy):
        x = []
        for q in range(8):
            rows = pl.ds(pl.multiple_of(q * 64 + oy * 8, 8), 8)
            value = (mid[rows, 0:128], mid[rows, 128:256])
            if q:
                value = times(value, turn_one[0, kt, q], turn_one[1, kt, q], -1)
            x.append(value)
        for k, value in enumerate(eight(x, -1)):
            value = times(value, moved[0, kt, oy, k], moved[1, kt, oy, k], -1)
            work[0, k, oy] = value[0]
            work[1, k, oy] = value[1]

    @pl.loop(0, 8, unroll=2)
    def _(kq):
        x = eight([(work[0, kq, oy], work[1, kq, oy]) for oy in range(8)], -1)
        y = []
        for k in range(8):
            rows = pl.ds(pl.multiple_of((kt * 8 + k) * 64 + kq * 8, 8), 8)
            scale = factor[rows, :]
            y.append((x[k][0] * scale, x[k][1] * scale))
        for y0, value in enumerate(eight(y, 1)):
            value = times(value, turn_two[0, kt, y0, kq], turn_two[1, kt, y0, kq], 1)
            work[0, kq, y0] = value[0]
            work[1, kq, y0] = value[1]

    @pl.loop(0, 8, unroll=2)
    def _(y0):
        x = [(work[0, kq, y0], work[1, kq, y0]) for kq in range(8)]
        for y1, value in enumerate(eight(x, 1)):
            if y1:
                value = times(value, turn_one[0, kt, y1], turn_one[1, kt, y1], 1)
            placed[0, kt, y1, y0] = value[0]
            placed[1, kt, y1, y0] = value[1]


def next_digit(ktp, digits, placed, mixed):
    @pl.loop(0, 4, unroll=True)
    def _(pair):
        columns = []
        for one in range(2):
            pieces = [
                placed[part, 2 * ktp + k, 2 * pair + one].reshape(64, 128)
                for part in range(2)
                for k in range(2)
            ]
            columns.append(jnp.concatenate(pieces, axis=0))
        high, low = split(jnp.concatenate(columns, axis=1))
        both = dot(digits[ktp], high)
        mixed[ktp, pair] = both[:256] + both[256:] + dot(digits[ktp, 0:256], low)


def last_digit(odd, mixed, lined):
    @pl.loop(0, 4, unroll=True)
    def _(pair):
        for y2a in range(odd, 8, 2):
            for one in range(2):
                x = []
                for kt in range(4):
                    base = (kt % 2) * 64 + y2a * 8
                    lanes = slice(one * 128, one * 128 + 128)
                    x.append((mixed[kt // 2, pair, base:base + 8, lanes],
                              mixed[kt // 2, pair, 128 + base:128 + base + 8, lanes]))
                for y2b, value in enumerate(four(x, 1)):
                    rows = pl.ds(pl.multiple_of((y2b * 8 + y2a) * 64 + (2 * pair + one) * 8, 8), 8)
                    lined[rows, 0:128] = value[0]
                    lined[rows, 128:256] = value[1]


PHASES = ((0, 3), (3, 1))


def whole_kernel(top, one, mixing, *refs):
    picks, refs = refs[:3], refs[3:]
    (turns, three, two_far, digits_far, slots_far, transfer, ahead_far, back_far, turn_one_far, turn_two_far,
     moved_far, out,
     first_map, second_map, leaf_map, two, digits, draws, parents, leaves, high_rows, low_rows, sent, arrived,
     slots, modes, factor, ahead, back, turn_one, turn_two, moved, flat, mid, work, placed, mixed, lined, ready,
          draw_sem, fetch_sem, send_sem, recv_sem, back_send, back_recv,
     two_sem) = refs
    row, col = lax.axis_index("row"), lax.axis_index("col")
    me = row * 16 + col
    core, z, y_low = lax.rem(col, 2), lax.rem(col // 2, 4), col // 8
    x, y_high = lax.rem(row, 4), row // 4

    digit = (lax.rem(col, 2) + 2 * lax.rem(col // 4, 2) + 4 * lax.rem(row, 2)
             + 8 * lax.rem(row // 4, 2))

    barrier = pltpu.get_barrier_semaphore()

    @pl.loop(1, 128)
    def _(k):
        other = lax.rem(me + k, 128)
        pl.semaphore_signal(barrier, inc=1, device_id=(other // 16, lax.rem(other, 16)),
                            device_id_type=MESH)

    def lanes_of(half):
        e = lax.rem(half + core, 2)
        return pl.ds(pl.multiple_of(e * 512, 512), 512)

    def draw_copy(half, tile):
        rows = pl.ds(pl.multiple_of(tile * 16, 16), 16)
        return pltpu.make_async_copy(three.at[:, rows, lanes_of(half)],
                                     draws.at[half, :, rows, :], draw_sem.at[half, tile])

    fetch_slots = pltpu.make_async_copy(slots_far.at[digit], slots, fetch_sem.at[6])
    fetch_slots.start()
    def two_copy(half):
        return pltpu.make_async_copy(two_far.at[:, lanes_of(half)], two.at[half], two_sem.at[half])

    def fetch_half(half):
        two_copy(half).start()
        for tile in range(4):
            draw_copy(half, tile).start()

    fetch_half(0)
    fetches = [
        pltpu.make_async_copy(transfer, modes, fetch_sem.at[0]),
        pltpu.make_async_copy(ahead_far.at[col], ahead, fetch_sem.at[1]),
        pltpu.make_async_copy(back_far.at[col], back, fetch_sem.at[4]),
        pltpu.make_async_copy(moved_far, moved, fetch_sem.at[5]),
        pltpu.make_async_copy(digits_far, digits, fetch_sem.at[7]),
        pltpu.make_async_copy(turn_one_far, turn_one, fetch_sem.at[2]),
        pltpu.make_async_copy(turn_two_far, turn_two, fetch_sem.at[3]),
    ]
    prepare(mixing, picks, first_map, second_map, leaf_map)
    fetch_slots.wait()

    def send(half, phase):
        first, count = PHASES[phase]
        kts = pl.ds(first, count)
        e = lax.rem(half + core, 2)

        @pl.loop(0, 64)
        def _(k):
            j = lax.rem(k * 21 + 21, 64)
            to_x = lax.rem(x + lax.rem(j, 4), 4)
            to_z = lax.rem(z + lax.rem(j // 4, 4), 4)
            to_y = lax.rem(y_low + lax.rem(j // 16, 2), 2)
            to_core = lax.rem(core + j // 32, 2)
            to_row, to_col = 4 * e + to_x, to_y * 8 + to_z * 2 + to_core
            here = jnp.logical_and(to_row == row, to_col == col)

            @pl.when(jnp.logical_not(here))
            def _():
                pltpu.make_async_remote_copy(
                    sent.at[half, to_x, to_col, kts], arrived.at[me, kts],
                    send_sem.at[half, phase], recv_sem.at[phase],
                    device_id=(to_row, to_col), device_id_type=MESH).start()

            @pl.when(here)
            def _():
                pltpu.make_async_copy(sent.at[half, to_x, to_col, kts], arrived.at[me, kts],
                                      send_sem.at[half, phase]).start()

    def sent_all(half, phase):
        first, count = PHASES[phase]
        view = sent.at[half, :, :, pl.ds(first, count)]
        pltpu.make_async_copy(view, view, send_sem.at[half, phase]).wait()

    def received_all(phase):
        first, count = PHASES[phase]
        view = arrived.at[pl.ds(0, 127), pl.ds(first, count)]
        pltpu.make_async_copy(view, view, recv_sem.at[phase]).wait()

    for half in range(2):
        two_copy(half).wait()
        expand(half, digit, lanes_of(half), top, one, two, draws, draw_copy, first_map, second_map,
               leaf_map, slots, turns, parents, leaves, high_rows, low_rows, sent, fetch_half)
        if half == 0:
            pl.semaphore_wait(barrier, 127)
        send(half, 0)
        if half == 0:
            for fetch in fetches:
                fetch.start()

    for fetch in fetches:
        fetch.wait()

    @pl.loop(0, 128)
    def _(i):
        low, kt, high = i // 32, lax.rem(i // 8, 4), lax.rem(i, 8)
        rows = modes[pl.ds(pl.multiple_of((low * 4 + kt) * 128 + high * 16, 16), 16), :]
        factor[pl.ds((kt * 8 + high) * 64 + low, 16, stride=4), :] = rows * (1.0 / (2048 * 2048))

    sent_all(0, 0)
    send(0, 1)
    sent_all(1, 0)
    send(1, 1)

    lane = lax.broadcasted_iota(jnp.int32, (8, 128), 1)
    for phase in range(2):
        if phase:
            sent_all(0, 1)
            sent_all(1, 1)
        received_all(phase)
        first, count = PHASES[phase]

        @pl.loop(first, first + count)
        def _(kt):
            along_lines(kt, arrived, factor, ahead, turn_one, turn_two, moved, lane, flat, mid, work,
                        placed)

        next_digit(phase, digits, placed, mixed)

    for odd in range(2):
        last_digit(odd, mixed, lined)
        half_strip = pl.ds(odd * 64, 64)

        @pl.loop(0, 16)
        def _(k):
            j = lax.rem(k * 7 + 7, 16)
            to_z = lax.rem(z + lax.rem(j // 2, 4), 4)
            to_y = lax.rem(y_low + lax.rem(j, 2), 2)
            to_core = lax.rem(core + j // 8, 2)
            to = to_y * 8 + to_z * 2 + to_core
            rows = pl.ds(pl.multiple_of(to * 128 + odd * 64, 64), 64)
            high, low = split(lined[rows, :])
            both = dot_nt(jnp.concatenate([high, low], axis=0), back[0])
            done = both[:64] + both[64:] + dot_nt(high, back[1])
            ready[to, 0, half_strip, :] = done[:, :128]
            ready[to, 1, half_strip, :] = done[:, 128:]
            source = ready.at[to, :, half_strip, :]
            target = out.at[col, :, half_strip, :]

            @pl.when(to != col)
            def _():
                pltpu.make_async_remote_copy(
                    source, target, back_send.at[odd], back_recv.at[odd],
                    device_id=(row, to), device_id_type=MESH).start()

            @pl.when(to == col)
            def _():
                pltpu.make_async_copy(source, target, back_send.at[odd]).start()

    for odd in range(2):
        half_strip = pl.ds(odd * 64, 64)
        view = ready.at[:, :, half_strip, :]
        pltpu.make_async_copy(view, view, back_send.at[odd]).wait()
        view = ready.at[pl.ds(0, 15), :, half_strip, :]
        pltpu.make_async_copy(view, view, back_recv.at[odd]).wait()


def strip_kernel(arrived, out, near, strip, sem, out_sem):
    def fetch(part):
        rows = pl.ds(part * 32, 32)
        return [
            pltpu.make_async_copy(arrived.at[pl.ds(8 * k, 8), :, rows, :],
                                  near.at[pl.ds(8 * k, 8), :, rows, :], sem.at[part, k])
            for k in range(2)
        ]

    def put(part):
        rows = pl.ds(part * 32, 32)
        return [
            pltpu.make_async_copy(strip.at[plane, rows, :], out.at[plane, rows, :],
                                  out_sem.at[part, plane])
            for plane in range(2)
        ]

    for part in range(4):
        for copy in fetch(part):
            copy.start()
    for part in range(4):
        for copy in fetch(part):
            copy.wait()

        @pl.loop(0, 4, unroll=2)
        def _(tile):
            rows = pl.ds(pl.multiple_of(part * 32 + tile * 8, 8), 8)
            x = [(near[k, 0, rows, :], near[k, 1, rows, :]) for k in range(16)]
            for place, value in enumerate(sixteen(x, 1)):
                strip[0, rows, place * 128:(place + 1) * 128] = value[0]
                strip[1, rows, place * 128:(place + 1) * 128] = value[1]

        for copy in put(part):
            copy.start()
    for part in range(4):
        for copy in put(part):
            copy.wait()


def body(*arrays):
    outside = pl.BlockSpec(memory_space=pl.ANY)
    return pl.pallas_call(
        strip_kernel,
        in_specs=[outside],
        out_specs=outside,
        out_shape=jax.ShapeDtypeStruct((2, 128, 2048), F32),
        scratch_shapes=[
            VMEM((16, 2, 128, 128), F32),
            VMEM((2, 128, 2048), F32),
            pltpu.SemaphoreType.DMA((4, 2)),
            pltpu.SemaphoreType.DMA((4, 2)),
        ],
        compiler_params=pltpu.CompilerParams(vmem_limit_bytes=60 * 2**20),
    )(whole(*arrays))


def whole(top, one, two, three, mixing, transfer):
    slots, turns = slot_tables()
    turn_one, turn_two, moved = turn_tables()
    ahead, back = line_tables()
    near = [top, one, mixing] + owner_tables()
    near += [turns]
    far = [three, two.reshape(448, 1024), digit_tables(), slots, transfer, ahead, back, turn_one, turn_two, moved]
    inside, outside = pl.BlockSpec(memory_space=VMEM), pl.BlockSpec(memory_space=pl.ANY)
    dma = pltpu.SemaphoreType.DMA
    return pl.pallas_call(
        whole_kernel,
        in_specs=[inside] * len(near) + [outside] * len(far),
        out_specs=outside,
        out_shape=jax.ShapeDtypeStruct((16, 2, 128, 128), F32),
        scratch_shapes=[
            VMEM((64, 64), BF16),
            VMEM((512, 512), BF16),
            VMEM((128, 1024), BF16),
            VMEM((2, 448, 512), BF16),
            VMEM((2, 512, 256), BF16),
            VMEM((2, 56, 64, 512), BF16),
            VMEM((4, 256, 512), BF16),
            VMEM((2, 2, 8, 8, 512), F32),
            VMEM((4, 256, 256), BF16),
            VMEM((4, 256, 256), BF16),
            VMEM((2, 4, 16, 4, 8, 128), F32),
            VMEM((128, 4, 8, 128), F32),
            VMEM((256, 256), BF16),
            VMEM((2048, 128), F32),
            VMEM((2056, 128), F32),
            VMEM((2, 256, 256), BF16),
            VMEM((2, 256, 256), BF16),
            VMEM((2, 4, 8, 8, 128), F32),
            VMEM((2, 4, 8, 8, 8, 128), F32),
            VMEM((2, 4, 8, 8, 8, 128), F32),
            VMEM((512, 256), F32),
            VMEM((512, 256), F32),
            VMEM((2, 8, 8, 8, 128), F32),
            VMEM((2, 4, 8, 8, 8, 128), F32),
            VMEM((2, 4, 256, 256), F32),
            VMEM((2048, 256), F32),
            VMEM((16, 2, 128, 128), F32),
            dma((2, 4)),
            dma((8,)),
            dma((2, 2)),
            dma((2,)),
            dma((2,)),
            dma((2,)),
            dma((2,)),
        ],
        compiler_params=pltpu.CompilerParams(
            collective_id=0, has_side_effects=True, vmem_limit_bytes=56 * 2**20),
    )(*[jnp.asarray(a) for a in near + far])


def solution(mesh):
    return jax.shard_map(
        body,
        mesh=mesh,
        in_specs=(
            P(None, ("row", "col")),
            P(None, ("row", "col")),
            P(None, None, ("row", "col")),
            P(None, None, ("row", "col")),
            P(),
            P(None, "col"),
        ),
        out_specs=P("row", "col", None),
        check_vma=False,
    )
```

```python
import math

import jax
import jax.numpy as jnp
import numpy as np
from jax import lax
from jax.experimental import pallas as pl
from jax.experimental.pallas import tpu as pltpu
from jax.sharding import PartitionSpec as P

F32 = jnp.float32
BF16 = jnp.bfloat16
VMEM = pltpu.VMEM
MESH = pl.DeviceIdType.MESH


def two_terms(values):
    values = np.asarray(values, np.float32)
    high = values.astype(jnp.bfloat16)
    low = (values - high.astype(np.float32)).astype(jnp.bfloat16)
    return high, low


def bit(value, index):
    return (value >> index) & 1


def owner_tables():
    row = np.arange(64)
    pick_one = np.zeros((64, 64), np.float32)
    pick_one[row, 8 * (row % 8) + row // 8] = 1
    row = np.arange(512)
    pick_two = np.zeros((512, 64), np.float32)
    pick_two[row, 8 * (row % 8) + ((row >> 4) & 7)] = 1
    row = np.arange(128)
    pick_three = np.zeros((128, 64), np.float32)
    pick_three[row, 8 * (4 * bit(row, 5) + 2 * bit(row, 3) + bit(row, 0))] = 1
    return [np.asarray(each, jnp.bfloat16) for each in (pick_one, pick_two, pick_three)]


def slot_tables():
    slot = np.arange(128)
    y_part = 2 * (slot // 32) + slot % 2
    z_part = (slot // 2) % 16
    mode = np.arange(128)
    kz, ky = mode // 8, mode % 8
    angle = np.outer(kz, z_part) / 16 + np.outer(ky, y_part) / 8
    angle = 2 * np.pi * (angle[None] + kz[None, :, None] * np.arange(16)[:, None, None] / 256)
    high, low = two_terms(np.concatenate([np.cos(angle), np.sin(angle)], axis=2))
    both = np.concatenate([high, low], axis=1)
    turn = 2 * np.pi * np.outer(np.arange(4), y_part) / 32
    turns = np.stack([np.cos(turn), np.sin(turn)]).astype(np.float32)
    return both, turns


def line_tables():
    z_low, kz_high = np.arange(128), np.arange(128)
    sign = 1 - 2 * (kz_high % 2)
    ahead, back = [], []
    for kz_low in range(16):
        angle = 2 * np.pi * np.outer(z_low, kz_low + 16 * kz_high) / 2048
        cos, sin = np.cos(angle), np.sin(angle)
        back.append(np.block([[cos, -sin], [sin, cos]]))
        angle = np.outer(z_low, kz_high) / 128 + (z_low % 8)[:, None] * kz_low / 2048
        cos, sin = np.cos(2 * np.pi * angle), np.sin(2 * np.pi * angle)
        ahead.append(np.block([[cos, -sin], [sin * sign, cos * sign]]))
    pair = lambda a: np.stack(two_terms(np.stack(a)), axis=1)
    return pair(ahead), pair(back)


def turn_tables():
    kt = np.arange(4)[:, None]
    s = np.arange(8)[None, :]
    ky_low = kt + 4 * s
    one = 2 * np.pi * ky_low[:, None, :] * np.arange(8)[None, :, None] / 256
    mode = ky_low[:, None, None, :] + 32 * np.arange(8)[None, None, :, None]
    two = 2 * np.pi * mode * np.arange(8)[None, :, None, None] / 2048
    wide = lambda a: np.ascontiguousarray(
        np.broadcast_to(np.stack([np.cos(a), np.sin(a)])[..., None], (2,) + a.shape + (128,))
    ).astype(np.float32)
    moved = two[..., None] - 2 * np.pi * np.multiply.outer(np.arange(8), np.arange(128))[
        None, :, None, None, :] / 16
    moved = np.stack([np.cos(moved), np.sin(moved)]).astype(np.float32)
    return wide(one), wide(two), moved


def digit_tables():
    out = []
    for pair in range(2):
        full = np.zeros((2, 2, 8, 8, 2, 2, 8, 8))
        for k in range(2):
            y2a = np.arange(8)[:, None]
            s = np.arange(8)[None, :]
            angle = 2 * np.pi * (s * y2a / 8 + (2 * pair + k) * y2a / 32)
            cos, sin = np.cos(angle), np.sin(angle)
            for y0 in range(8):
                full[0, k, :, y0, 0, k, y0, :] = cos
                full[0, k, :, y0, 1, k, y0, :] = -sin
                full[1, k, :, y0, 0, k, y0, :] = sin
                full[1, k, :, y0, 1, k, y0, :] = cos
        high, low = two_terms(full.reshape(256, 256))
        out.append(np.concatenate([high, low], axis=0))
    return np.stack(out)


def split(x):
    high = x.astype(BF16)
    return high, (x - high.astype(F32)).astype(BF16)


def dot(a, b):
    return jnp.dot(a, b, preferred_element_type=F32)


def dot_nt(a, b):
    return lax.dot_general(a, b, (((1,), (1,)), ((), ())), preferred_element_type=F32)


def add(a, b):
    return (a[0] + b[0], a[1] + b[1])


def sub(a, b):
    return (a[0] - b[0], a[1] - b[1])


def times(a, cos, sin, sign):
    if sign > 0:
        return (a[0] * cos - a[1] * sin, a[1] * cos + a[0] * sin)
    return (a[0] * cos + a[1] * sin, a[1] * cos - a[0] * sin)


def quarter(a, sign):
    return (-a[1], a[0]) if sign > 0 else (a[1], -a[0])


def add_quarter(a, b, sign):
    return (a[0] - b[1], a[1] + b[0]) if sign > 0 else (a[0] + b[1], a[1] - b[0])


def four(x, sign):
    even, odd = add(x[0], x[2]), add(x[1], x[3])
    left, right = sub(x[0], x[2]), sub(x[1], x[3])
    return [add(even, odd), add_quarter(left, right, sign), sub(even, odd),
            add_quarter(left, right, -sign)]


def eight(x, sign):
    even = four([x[0], x[2], x[4], x[6]], sign)
    odd = four([x[1], x[3], x[5], x[7]], sign)
    half = math.sqrt(0.5)
    a = odd[1]
    if sign > 0:
        odd1 = ((a[0] - a[1]) * half, (a[1] + a[0]) * half)
    else:
        odd1 = ((a[0] + a[1]) * half, (a[1] - a[0]) * half)
    a = odd[3]
    if sign > 0:
        odd3 = ((-a[0] - a[1]) * half, (a[0] - a[1]) * half)
    else:
        odd3 = ((a[1] - a[0]) * half, (-a[0] - a[1]) * half)
    return [
        add(even[0], odd[0]),
        add(even[1], odd1),
        add_quarter(even[2], odd[2], sign),
        add(even[3], odd3),
        sub(even[0], odd[0]),
        sub(even[1], odd1),
        add_quarter(even[2], odd[2], -sign),
        sub(even[3], odd3),
    ]


def sixteen(x, sign):
    out = [None] * 16
    mid = [four([x[a], x[a + 4], x[a + 8], x[a + 12]], sign) for a in range(4)]
    for c in range(4):
        terms = []
        for a in range(4):
            angle = 2 * math.pi * a * c / 16
            if a * c == 0:
                terms.append(mid[a][c])
            elif a * c == 4:
                terms.append(quarter(mid[a][c], sign))
            else:
                terms.append(times(mid[a][c], math.cos(angle), math.sin(angle), sign))
        done = four(terms, sign)
        for d in range(4):
            out[c + 4 * d] = done[d]
    return out


def spread(rows, width, own):
    shape = (64, 64 * width)
    column = lax.broadcasted_iota(jnp.int32, shape, 1) // width
    source = lax.broadcasted_iota(jnp.int32, shape, 0)
    wide = dot(rows.astype(BF16), (((column + 8) & 63) == source).astype(F32).astype(BF16))
    shape = (rows.shape[0], 64 * width)
    cell = lax.broadcasted_iota(jnp.int32, shape, 1) & (width - 1)
    return jnp.where(cell == own(lax.broadcasted_iota(jnp.int32, shape, 0)), wide, 0.0).astype(BF16)


def prepare(mixing, picks, first_map, second_map, leaf_map):
    mix = mixing[...]
    first_map[...] = dot(picks[0][...], mix).astype(BF16)
    second_map[...] = spread(dot(picks[1][...], mix), 8, lambda r: 2 * (r >> 7) + bit(r, 3))
    leaf_map[...] = spread(
        dot(picks[2][...], mix), 16,
        lambda r: 8 * bit(r, 2) + 4 * bit(r, 6) + 2 * bit(r, 4) + bit(r, 1))


def expand(half, digit, lanes, top, one, two, draws, arrived_draws, first_map, second_map, leaf_map,
           slots, turns, parents, leaves, high_rows, low_rows, sent, fetch_half):
    records = jnp.concatenate([top[:, lanes], one[:, lanes].astype(F32)], axis=0)
    high, low = split(records)
    high, low = split(dot(first_map[...], high) + dot(first_map[...], low))
    level_two = dot(second_map[...], jnp.concatenate([two[half], high], axis=0))
    low = jnp.concatenate([jnp.zeros_like(low), low], axis=0)
    level_two = level_two + dot(second_map[:, 384:], low)
    for tile in range(4):
        high, low = split(level_two[tile * 128:(tile + 1) * 128])
        parents[tile, 0:128] = high
        parents[tile, 128:256] = low

    if half == 0:
        fetch_half(1)

    @pl.loop(0, 2)
    def _(c1x):
        for c1y in range(2):
            tile = 2 * c1x + c1y
            arrived_draws(half, tile).wait()
            rows = pl.ds(pl.multiple_of(tile * 16, 16), 16)
            got = dot(leaf_map[:, :896], draws[half, :, rows, :].reshape(896, 512))
            near = parents[tile]
            got = got + dot(leaf_map[:, 896:], near[:128]) + dot(leaf_map[:, 896:], near[128:])
            for group in range(4):
                for i in range(4):
                    row = group * 32 + i * 8
                    leaves[group // 2, group % 2, 4 * c1y + i] = got[row:row + 8]

        @pl.loop(0, 8, unroll=4)
        def _(twin):
            for pair in range(2):
                quarters = []
                for t in range(4):
                    lane = slice(t * 128, t * 128 + 128)
                    first, second = [], []
                    for j in range(2):
                        group = lax.rem(2 * twin + j - digit + 16, 16)
                        part, oy = group // 8, lax.rem(group, 8)
                        first.append(leaves[pair, part, oy, :, lane])
                        other = leaves[pair, 1 - part, oy, :, lane]
                        second.append(other * (1 - 2 * part).astype(F32))
                    quarters.append((jnp.concatenate(first, axis=0), jnp.concatenate(second, axis=0)))
                rows = pl.ds(pl.multiple_of(pair * 128 + twin * 16, 16), 16)
                for k, value in enumerate(four(quarters, -1)):
                    if k:
                        value = times(value, turns[0, k:k + 1], turns[1, k:k + 1], -1)
                    for side in range(2):
                        high, low = split(value[side])
                        high_rows[k, rows, side * 128:side * 128 + 128] = high
                        low_rows[k, rows, side * 128:side * 128 + 128] = low

        for k in range(4):
            both = dot_nt(slots[...], high_rows[k])
            done = both[:128] + both[128:] + dot_nt(slots[0:128], low_rows[k])
            for pair in range(2):
                piece = done[:, pair * 128:(pair + 1) * 128].reshape(16, 8, 128)
                sent[half, 2 * c1x + pair, :, k] = piece


def owner_index(q, w):
    index = 0
    for b in range(4):
        index += bit(w, b) << (2 * b)
    for b in range(3):
        index += bit(q, b) << (2 * b + 1)
    return index


def gather_lanes(x, lane):
    for b in range(4):
        here = (lane & (8 << b)) != 0
        x = [jnp.where(here, x[(m + (1 << b)) % 16], x[m]) for m in range(16)]
    return [x[(16 - d) % 16] for d in range(16)]


def along_lines(kt, arrived, factor, table, turn_one, turn_two, moved, lane, flat, mid, work, placed):
    @pl.loop(0, 8, unroll=2)
    def _(q):
        base = 2 * (q % 2) + 8 * ((q // 2) % 2) + 32 * (q // 4)
        places = [owner_index(0, w) for w in range(16)]
        got = gather_lanes([arrived[base + place, kt] for place in places], lane)
        for oy in range(8):
            rows = pl.ds(pl.multiple_of(q * 64 + oy * 8, 8), 8)
            flat[rows, 0:128] = got[oy]
            flat[rows, 128:256] = got[8 + oy]

    for part in range(2):
        rows = pl.ds(part * 256, 256)
        high, low = split(flat[rows, :])
        mid[rows, :] = dot(high, table[0]) + dot(low, table[0]) + dot(high, table[1])

    @pl.loop(0, 8, unroll=2)
    def _(oy):
        x = []
        for q in range(8):
            rows = pl.ds(pl.multiple_of(q * 64 + oy * 8, 8), 8)
            value = (mid[rows, 0:128], mid[rows, 128:256])
            if q:
                value = times(value, turn_one[0, kt, q], turn_one[1, kt, q], -1)
            x.append(value)
        for k, value in enumerate(eight(x, -1)):
            value = times(value, moved[0, kt, oy, k], moved[1, kt, oy, k], -1)
            work[0, k, oy] = value[0]
            work[1, k, oy] = value[1]

    @pl.loop(0, 8, unroll=2)
    def _(kq):
        x = eight([(work[0, kq, oy], work[1, kq, oy]) for oy in range(8)], -1)
        y = []
        for k in range(8):
            rows = pl.ds(pl.multiple_of((kt * 8 + k) * 64 + kq * 8, 8), 8)
            scale = factor[rows, :]
            y.append((x[k][0] * scale, x[k][1] * scale))
        for y0, value in enumerate(eight(y, 1)):
            value = times(value, turn_two[0, kt, y0, kq], turn_two[1, kt, y0, kq], 1)
            work[0, kq, y0] = value[0]
            work[1, kq, y0] = value[1]

    @pl.loop(0, 8, unroll=2)
    def _(y0):
        x = [(work[0, kq, y0], work[1, kq, y0]) for kq in range(8)]
        for y1, value in enumerate(eight(x, 1)):
            if y1:
                value = times(value, turn_one[0, kt, y1], turn_one[1, kt, y1], 1)
            placed[0, kt, y1, y0] = value[0]
            placed[1, kt, y1, y0] = value[1]


def next_digit(ktp, digits, placed, mixed):
    @pl.loop(0, 4, unroll=True)
    def _(pair):
        columns = []
        for one in range(2):
            pieces = [
                placed[part, 2 * ktp + k, 2 * pair + one].reshape(64, 128)
                for part in range(2)
                for k in range(2)
            ]
            columns.append(jnp.concatenate(pieces, axis=0))
        high, low = split(jnp.concatenate(columns, axis=1))
        both = dot(digits[ktp], high)
        mixed[ktp, pair] = both[:256] + both[256:] + dot(digits[ktp, 0:256], low)


def last_digit(odd, mixed, lined):
    @pl.loop(0, 4, unroll=True)
    def _(pair):
        for y2a in range(odd, 8, 2):
            for one in range(2):
                x = []
                for kt in range(4):
                    base = (kt % 2) * 64 + y2a * 8
                    lanes = slice(one * 128, one * 128 + 128)
                    x.append((mixed[kt // 2, pair, base:base + 8, lanes],
                              mixed[kt // 2, pair, 128 + base:128 + base + 8, lanes]))
                for y2b, value in enumerate(four(x, 1)):
                    rows = pl.ds(pl.multiple_of((y2b * 8 + y2a) * 64 + (2 * pair + one) * 8, 8), 8)
                    lined[rows, 0:128] = value[0]
                    lined[rows, 128:256] = value[1]


PHASES = ((0, 3), (3, 1))


def whole_kernel(top, one, mixing, *refs):
    picks, refs = refs[:3], refs[3:]
    (turns, three, two_far, digits_far, slots_far, transfer, ahead_far, back_far, turn_one_far, turn_two_far,
     moved_far, out,
     first_map, second_map, leaf_map, two, digits, draws, parents, leaves, high_rows, low_rows, sent, arrived,
     slots, modes, factor, ahead, back, turn_one, turn_two, moved, flat, mid, work, placed, mixed, lined, ready,
          draw_sem, fetch_sem, send_sem, recv_sem, back_send, back_recv,
     two_sem) = refs
    row, col = lax.axis_index("row"), lax.axis_index("col")
    me = row * 16 + col
    core, z, y_low = lax.rem(col, 2), lax.rem(col // 2, 4), col // 8
    x, y_high = lax.rem(row, 4), row // 4

    digit = (lax.rem(col, 2) + 2 * lax.rem(col // 4, 2) + 4 * lax.rem(row, 2)
             + 8 * lax.rem(row // 4, 2))

    barrier = pltpu.get_barrier_semaphore()

    @pl.loop(1, 128)
    def _(k):
        other = lax.rem(me + k, 128)
        pl.semaphore_signal(barrier, inc=1, device_id=(other // 16, lax.rem(other, 16)),
                            device_id_type=MESH)

    def lanes_of(half):
        e = lax.rem(half + core, 2)
        return pl.ds(pl.multiple_of(e * 512, 512), 512)

    def draw_copy(half, tile):
        rows = pl.ds(pl.multiple_of(tile * 16, 16), 16)
        return pltpu.make_async_copy(three.at[:, rows, lanes_of(half)],
                                     draws.at[half, :, rows, :], draw_sem.at[half, tile])

    fetch_slots = pltpu.make_async_copy(slots_far.at[digit], slots, fetch_sem.at[6])
    fetch_slots.start()
    def two_copy(half):
        return pltpu.make_async_copy(two_far.at[:, lanes_of(half)], two.at[half], two_sem.at[half])

    def fetch_half(half):
        two_copy(half).start()
        for tile in range(4):
            draw_copy(half, tile).start()

    fetch_half(0)
    fetches = [
        pltpu.make_async_copy(transfer, modes, fetch_sem.at[0]),
        pltpu.make_async_copy(ahead_far.at[col], ahead, fetch_sem.at[1]),
        pltpu.make_async_copy(back_far.at[col], back, fetch_sem.at[4]),
        pltpu.make_async_copy(moved_far, moved, fetch_sem.at[5]),
        pltpu.make_async_copy(digits_far, digits, fetch_sem.at[7]),
        pltpu.make_async_copy(turn_one_far, turn_one, fetch_sem.at[2]),
        pltpu.make_async_copy(turn_two_far, turn_two, fetch_sem.at[3]),
    ]
    prepare(mixing, picks, first_map, second_map, leaf_map)
    fetch_slots.wait()

    def send(half, phase):
        first, count = PHASES[phase]
        kts = pl.ds(first, count)
        e = lax.rem(half + core, 2)

        @pl.loop(0, 64)
        def _(k):
            j = lax.rem(k * 21 + 21, 64)
            to_x = lax.rem(x + lax.rem(j, 4), 4)
            to_z = lax.rem(z + lax.rem(j // 4, 4), 4)
            to_y = lax.rem(y_low + lax.rem(j // 16, 2), 2)
            to_core = lax.rem(core + j // 32, 2)
            to_row, to_col = 4 * e + to_x, to_y * 8 + to_z * 2 + to_core
            here = jnp.logical_and(to_row == row, to_col == col)

            @pl.when(jnp.logical_not(here))
            def _():
                pltpu.make_async_remote_copy(
                    sent.at[half, to_x, to_col, kts], arrived.at[me, kts],
                    send_sem.at[half, phase], recv_sem.at[phase],
                    device_id=(to_row, to_col), device_id_type=MESH).start()

            @pl.when(here)
            def _():
                pltpu.make_async_copy(sent.at[half, to_x, to_col, kts], arrived.at[me, kts],
                                      send_sem.at[half, phase]).start()

    def sent_all(half, phase):
        first, count = PHASES[phase]
        view = sent.at[half, :, :, pl.ds(first, count)]
        pltpu.make_async_copy(view, view, send_sem.at[half, phase]).wait()

    def received_all(phase):
        first, count = PHASES[phase]
        view = arrived.at[pl.ds(0, 127), pl.ds(first, count)]
        pltpu.make_async_copy(view, view, recv_sem.at[phase]).wait()

    for half in range(2):
        two_copy(half).wait()
        expand(half, digit, lanes_of(half), top, one, two, draws, draw_copy, first_map, second_map,
               leaf_map, slots, turns, parents, leaves, high_rows, low_rows, sent, fetch_half)
        if half == 0:
            pl.semaphore_wait(barrier, 127)
        send(half, 0)
        if half == 0:
            for fetch in fetches:
                fetch.start()

    for fetch in fetches:
        fetch.wait()

    @pl.loop(0, 128)
    def _(i):
        low, kt, high = i // 32, lax.rem(i // 8, 4), lax.rem(i, 8)
        rows = modes[pl.ds(pl.multiple_of((low * 4 + kt) * 128 + high * 16, 16), 16), :]
        factor[pl.ds((kt * 8 + high) * 64 + low, 16, stride=4), :] = rows * (1.0 / (2048 * 2048))

    sent_all(0, 0)
    send(0, 1)
    sent_all(1, 0)
    send(1, 1)

    lane = lax.broadcasted_iota(jnp.int32, (8, 128), 1)
    for phase in range(2):
        if phase:
            sent_all(0, 1)
            sent_all(1, 1)
        received_all(phase)
        first, count = PHASES[phase]

        @pl.loop(first, first + count)
        def _(kt):
            along_lines(kt, arrived, factor, ahead, turn_one, turn_two, moved, lane, flat, mid, work,
                        placed)

        next_digit(phase, digits, placed, mixed)

    for odd in range(2):
        last_digit(odd, mixed, lined)
        half_strip = pl.ds(odd * 64, 64)

        @pl.loop(0, 16)
        def _(k):
            j = lax.rem(k * 7 + 7, 16)
            to_z = lax.rem(z + lax.rem(j // 2, 4), 4)
            to_y = lax.rem(y_low + lax.rem(j, 2), 2)
            to_core = lax.rem(core + j // 8, 2)
            to = to_y * 8 + to_z * 2 + to_core
            rows = pl.ds(pl.multiple_of(to * 128 + odd * 64, 64), 64)
            high, low = split(lined[rows, :])
            both = dot_nt(jnp.concatenate([high, low], axis=0), back[0])
            done = both[:64] + both[64:] + dot_nt(high, back[1])
            ready[to, 0, half_strip, :] = done[:, :128]
            ready[to, 1, half_strip, :] = done[:, 128:]
            source = ready.at[to, :, half_strip, :]
            target = out.at[col, :, half_strip, :]

            @pl.when(to != col)
            def _():
                pltpu.make_async_remote_copy(
                    source, target, back_send.at[odd], back_recv.at[odd],
                    device_id=(row, to), device_id_type=MESH).start()

            @pl.when(to == col)
            def _():
                pltpu.make_async_copy(source, target, back_send.at[odd]).start()

    for odd in range(2):
        half_strip = pl.ds(odd * 64, 64)
        view = ready.at[:, :, half_strip, :]
        pltpu.make_async_copy(view, view, back_send.at[odd]).wait()
        view = ready.at[pl.ds(0, 15), :, half_strip, :]
        pltpu.make_async_copy(view, view, back_recv.at[odd]).wait()


def strip_kernel(arrived, out, near, strip, sem, out_sem):
    def fetch(part):
        rows = pl.ds(part * 16, 16)
        return [
            pltpu.make_async_copy(arrived.at[pl.ds(8 * k, 8), :, rows, :],
                                  near.at[pl.ds(8 * k, 8), :, rows, :], sem.at[part, k])
            for k in range(2)
        ]

    def put(part):
        rows = pl.ds(part * 16, 16)
        return [
            pltpu.make_async_copy(strip.at[plane, rows, :], out.at[plane, rows, :],
                                  out_sem.at[part, plane])
            for plane in range(2)
        ]

    for part in range(8):
        for copy in fetch(part):
            copy.start()
    for part in range(8):
        for copy in fetch(part):
            copy.wait()

        @pl.loop(0, 2, unroll=2)
        def _(tile):
            rows = pl.ds(pl.multiple_of(part * 16 + tile * 8, 8), 8)
            x = [(near[k, 0, rows, :], near[k, 1, rows, :]) for k in range(16)]
            for place, value in enumerate(sixteen(x, 1)):
                strip[0, rows, place * 128:(place + 1) * 128] = value[0]
                strip[1, rows, place * 128:(place + 1) * 128] = value[1]

        for copy in put(part):
            copy.start()
    for part in range(8):
        for copy in put(part):
            copy.wait()


def body(*arrays):
    outside = pl.BlockSpec(memory_space=pl.ANY)
    return pl.pallas_call(
        strip_kernel,
        in_specs=[outside],
        out_specs=outside,
        out_shape=jax.ShapeDtypeStruct((2, 128, 2048), F32),
        scratch_shapes=[
            VMEM((16, 2, 128, 128), F32),
            VMEM((2, 128, 2048), F32),
            pltpu.SemaphoreType.DMA((8, 2)),
            pltpu.SemaphoreType.DMA((8, 2)),
        ],
        compiler_params=pltpu.CompilerParams(vmem_limit_bytes=60 * 2**20),
    )(whole(*arrays))


def whole(top, one, two, three, mixing, transfer):
    slots, turns = slot_tables()
    turn_one, turn_two, moved = turn_tables()
    ahead, back = line_tables()
    near = [top, one, mixing] + owner_tables()
    near += [turns]
    far = [three, two.reshape(448, 1024), digit_tables(), slots, transfer, ahead, back, turn_one, turn_two, moved]
    inside, outside = pl.BlockSpec(memory_space=VMEM), pl.BlockSpec(memory_space=pl.ANY)
    dma = pltpu.SemaphoreType.DMA
    return pl.pallas_call(
        whole_kernel,
        in_specs=[inside] * len(near) + [outside] * len(far),
        out_specs=outside,
        out_shape=jax.ShapeDtypeStruct((16, 2, 128, 128), F32),
        scratch_shapes=[
            VMEM((64, 64), BF16),
            VMEM((512, 512), BF16),
            VMEM((128, 1024), BF16),
            VMEM((2, 448, 512), BF16),
            VMEM((2, 512, 256), BF16),
            VMEM((2, 56, 64, 512), BF16),
            VMEM((4, 256, 512), BF16),
            VMEM((2, 2, 8, 8, 512), F32),
            VMEM((4, 256, 256), BF16),
            VMEM((4, 256, 256), BF16),
            VMEM((2, 4, 16, 4, 8, 128), F32),
            VMEM((128, 4, 8, 128), F32),
            VMEM((256, 256), BF16),
            VMEM((2048, 128), F32),
            VMEM((2056, 128), F32),
            VMEM((2, 256, 256), BF16),
            VMEM((2, 256, 256), BF16),
            VMEM((2, 4, 8, 8, 128), F32),
            VMEM((2, 4, 8, 8, 8, 128), F32),
            VMEM((2, 4, 8, 8, 8, 128), F32),
            VMEM((512, 256), F32),
            VMEM((512, 256), F32),
            VMEM((2, 8, 8, 8, 128), F32),
            VMEM((2, 4, 8, 8, 8, 128), F32),
            VMEM((2, 4, 256, 256), F32),
            VMEM((2048, 256), F32),
            VMEM((16, 2, 128, 128), F32),
            dma((2, 4)),
            dma((8,)),
            dma((2, 2)),
            dma((2,)),
            dma((2,)),
            dma((2,)),
            dma((2,)),
        ],
        compiler_params=pltpu.CompilerParams(
            collective_id=0, has_side_effects=True, vmem_limit_bytes=56 * 2**20),
    )(*[jnp.asarray(a) for a in near + far])


def solution(mesh):
    return jax.shard_map(
        body,
        mesh=mesh,
        in_specs=(
            P(None, ("row", "col")),
            P(None, ("row", "col")),
            P(None, None, ("row", "col")),
            P(None, None, ("row", "col")),
            P(),
            P(None, "col"),
        ),
        out_specs=P("row", "col", None),
        check_vma=False,
    )
```
